256 devices in a mesh: rows: 64 (over z, y, core), cols: 4 (over x).
Axes of the slice: x: 4, y: 4, z: 8, core: 2. Of those that a mesh axis runs over, the one named last changes fastest.
Arguments:
- tile_blocks: bfloat16 [2048, 8, 256, 256], P(('rows', 'cols')), may hold values from 0.049804688 to 1
- tile_cols: int32 [2048, 8], P(('rows', 'cols')), may hold values from 0 to 2047, as said below
- tile_count: int32 [2048], P(('rows', 'cols')), may hold values from 1 to 8
- start_mass: float32 [524288], P(('rows', 'cols')), may hold values from 0.5 to 64
- probe_block: bfloat16 [32, 524288], P(None, ('rows', 'cols')), may hold values from -6 to 6
Outputs:
- basis: float32 [32, 524288], P(None, ('rows', 'cols'))
The draws below stay inside these ranges and needn't reach their ends.
Inputs may be any that keep to these rules, and one draw needn't show every extreme that they name: `tile_cols`: slot 0 names the block row itself; every other slot names a block within 8 blocks of its row, cyclically over 2048.
All inputs are finite; a program needn't handle non-finite values.
Results may differ from the reference program's by a relative error of at most 0.00035.
The reference program's roundings to bfloat16 on the way count: a program that leaves them out, or rounds other values in their place, can miss the bound.
Values may be sent and summed in bfloat16 or wider, within the bound.
No kernel may reach another device: no remote copies, remote signals or barrier semaphores. Data moves between devices by JAX's collectives and lax.ppermute only.
A program may use at most 64 MiB of HBM per device.

```python
import math
import jax
import jax.numpy as jnp
from jax import lax

TILE = 256
K = 8
COLS = 32
BR_DEV = 8
POWER = 4
BLOCKS = 2048
ZONES = 524288


def draw_tile_cols(key, part):
    key = jax.random.fold_in(key, 7)
    offsets = jax.random.randint(key, (BLOCKS, K), -BR_DEV, BR_DEV + 1)
    slot_index = jnp.arange(K)[None, :]
    offsets = jnp.where(slot_index == 0, 0, offsets)
    base_rows = jnp.arange(BLOCKS)[:, None]
    return ((base_rows + offsets) % BLOCKS).astype(jnp.int32)


def rising_mass(rough, factor):
    place = jnp.arange(ZONES).astype(jnp.float32) / ZONES
    return (jnp.exp(jnp.log(factor) * place) * rough).astype(jnp.float32)


def draw_start_mass(key, part):
    key = jax.random.fold_in(key, 11)
    rough = jnp.exp(jax.random.uniform(key, (ZONES,), jnp.float32, jnp.log(0.5), jnp.log(2.0)))
    return rising_mass(rough, 8.0)


def set_ends(values, key, least, high):
    longest = values.shape.index(max(values.shape))
    spots = []
    for shift in (0, 1):
        where = [jax.random.randint(jax.random.fold_in(key, axis), (), 0, length) for axis, length in enumerate(values.shape)]
        where[longest] = (where[longest] + shift) % values.shape[longest]
        spots.append(tuple(where))
    return values.at[spots[0]].set(least).at[spots[1]].set(high)


def level_of(own_key, dims, split, least, largest):
    gain, own = 1.0, jax.random.fold_in(own_key, 6)
    for position, blocks in split:
        heights = jnp.exp(jax.random.uniform(jax.random.fold_in(own, position), (blocks,), jnp.float32, least / len(split), largest / len(split)))
        gain = gain * jnp.repeat(heights, dims[position] // blocks).reshape([-1 if axis == position else 1 for axis in range(len(dims))])
    return gain


def gaussian(own_key, extent, width, reach, shards=(), held_as=jnp.bfloat16):
    values = width * jax.random.normal(own_key, extent, jnp.float32)
    if shards:
        values = values * level_of(own_key, extent, shards, -0.22, 0.18)
    return jnp.clip(values, -reach, reach).astype(held_as)


def setup_inputs(seed: int = 0) -> dict:
    streams_of = jax.random.split(jax.random.key(seed), 6)
    return {
        "tile_blocks": jnp.clip(0.049804688 + 0.9501953 * jax.random.uniform(streams_of[0], (BLOCKS, K, TILE, TILE), jnp.float32) ** level_of(streams_of[0], (BLOCKS, K, TILE, TILE), ((0, 256),), -0.2, 0.2), 0.049804688, 1.0).astype(jnp.bfloat16),
        "tile_cols": draw_tile_cols(jax.random.fold_in(streams_of[5], 71), 0),
        "tile_count": set_ends(jax.random.randint(streams_of[2], (BLOCKS,), 1, K + 1), jax.random.fold_in(streams_of[2], 1), 1, K).astype(jnp.int32),
        "start_mass": draw_start_mass(jax.random.fold_in(streams_of[5], 71), 0),
        "probe_block": gaussian(streams_of[4], (COLS, ZONES), 1.0, 6.0, ((1, 256),)),
    }


def reference(tile_blocks, tile_cols, tile_count, start_mass, probe_block):
    highest = lax.Precision.HIGHEST
    live_slots = (jnp.arange(K)[None, :] < tile_count[:, None]).astype(jnp.float32)
    grouped = tile_blocks.reshape(BLOCKS // BR_DEV, BR_DEV, K, TILE, TILE)
    col_groups = tile_cols.reshape(BLOCKS // BR_DEV, BR_DEV, K)
    mask_groups = live_slots.reshape(BLOCKS // BR_DEV, BR_DEV, K)

    def row_part(group_tiles):
        return lax.optimization_barrier(jnp.sum(group_tiles.astype(jnp.float32), axis=3))
    partial_rows = lax.map(row_part, grouped).reshape(BLOCKS, K, TILE)
    row_sum = lax.optimization_barrier(jnp.sum(partial_rows * live_slots[:, :, None], axis=1))
    row_inverse = 1.0 / row_sum

    def transposed(weighted):
        chans = weighted.shape[0]
        w_groups = weighted.reshape(chans, BLOCKS // BR_DEV, BR_DEV, TILE).transpose(1, 0, 2, 3)

        def add_group(carried, items):
            group_tiles, group_w, group_cols, group_mask = items
            contrib = jnp.einsum('bkij,cbi->cbkj', group_tiles.astype(jnp.float32), group_w.astype(jnp.float32), precision=highest)
            contrib = contrib * group_mask[None, :, :, None]
            return (carried.at[:, group_cols.reshape(-1)].add(contrib.reshape(chans, BR_DEV * K, TILE)), None)
        result, ignored = lax.scan(add_group, jnp.zeros((chans, BLOCKS, TILE), jnp.float32), (grouped, w_groups, col_groups, mask_groups))
        return result

    def forward(operand):
        chans = operand.shape[0]

        def one_group(items):
            group_tiles, group_cols, group_mask = items
            gathered = operand[:, group_cols].astype(jnp.float32) * group_mask[None, :, :, None]
            return jnp.einsum('bkij,cbkj->cbi', group_tiles.astype(jnp.float32), gathered, precision=highest)
        result = lax.map(one_group, (grouped, col_groups, mask_groups))
        return result.transpose(1, 0, 2, 3).reshape(chans, BLOCKS, TILE)
    zone_root = math.sqrt(ZONES)
    stationary = start_mass.reshape(BLOCKS, TILE)
    for power_step in range(POWER):
        weighted = (stationary * row_inverse).astype(jnp.bfloat16)
        arrived = transposed(weighted[None])[0]
        raw_mass = 0.85 * arrived + 0.15
        stationary = raw_mass * zone_root / jnp.sqrt(jnp.sum(raw_mass * raw_mass))
    root_mass = jnp.sqrt(stationary)
    probe_rows = probe_block.reshape(COLS, BLOCKS, TILE).astype(jnp.float32)
    scaled_probe = (probe_rows / root_mass[None]).astype(jnp.bfloat16)
    forward_term = forward(scaled_probe) * (root_mass * row_inverse)[None]
    pushed = (probe_rows * (root_mass * row_inverse)[None]).astype(jnp.bfloat16)
    transposed_term = transposed(pushed) / root_mass[None]
    embedded = (0.5 * (forward_term + transposed_term)).reshape(COLS, ZONES)
    gram_matrix = jnp.dot(embedded, embedded.T, precision=highest)
    lower_factor = jnp.linalg.cholesky(gram_matrix)
    return jax.scipy.linalg.solve_triangular(lower_factor, embedded, lower=True)
```

```python
import math

import jax
import jax.numpy as jnp
from jax import lax
from jax.sharding import PartitionSpec as P

POWER = 4
RING = ("rows", "cols")
HIGHEST = lax.Precision.HIGHEST


def swap(shard, axis, partner):
    count = lax.axis_size(axis)
    return lax.ppermute(shard, axis, [(i, partner(i) % count) for i in range(count)])


def ring_pairs(shard_odd, shard_even):
    got_odd = swap(shard_odd, RING, lambda i: i + 1 if i % 2 else i - 1)
    got_even = swap(shard_even, RING, lambda i: i - 1 if i % 2 else i + 1)
    return got_odd, got_even


def all_sum(part):
    part = part + swap(part, "rows", lambda i: i ^ 1)
    part = part + sum(swap(part, "cols", lambda i, d=d: i ^ d) for d in (2, 1, 3))
    part = part + sum(swap(part, "rows", lambda i, d=d: i ^ d) for d in (4, 2, 6))
    part = part + swap(part, "rows", lambda i: i ^ 8)
    return part + sum(
        swap(part, "rows", lambda i, d=d: i + 8 * d if (i // 8) % 2 else i - 8 * d) for d in (3, 2, 1)
    )


def spread_rows(tile_blocks, weighted, place_table):
    chans = weighted.shape[0]
    blocks_dev, slot_count, tile_width = tile_blocks.shape[:3]
    contrib = jnp.einsum("bkij,cbi->cbkj", tile_blocks, weighted, preferred_element_type=jnp.float32)
    contrib = contrib.reshape(chans, blocks_dev * slot_count, tile_width)
    return jnp.einsum("wm,cmj->cwj", place_table, contrib, precision=HIGHEST)


def per_device(tile_blocks, tile_cols, tile_count, start_mass, probe_block):
    blocks_dev, slot_count, tile_width = tile_blocks.shape[:3]
    chans = probe_block.shape[0]
    devices = lax.axis_size(RING)
    total_blocks = blocks_dev * devices
    zones = total_blocks * tile_width
    zone_root = math.sqrt(zones)
    place = lax.axis_index(RING)
    odd = place % 2 == 1
    live_slots = (jnp.arange(slot_count)[None, :] < tile_count[:, None]).astype(jnp.float32)
    local_index = (tile_cols - place * blocks_dev + blocks_dev) % total_blocks
    place_table = (jnp.arange(3 * blocks_dev)[:, None] == local_index.reshape(-1)[None, :]).astype(jnp.float32)
    place_table = place_table * live_slots.reshape(-1)[None, :]
    partial_rows = jnp.sum(tile_blocks, axis=3, dtype=jnp.float32)
    row_sum = jnp.sum(partial_rows * live_slots[:, :, None], axis=1)
    row_inverse = 1.0 / row_sum

    def push(weighted, parts=1):
        window = spread_rows(tile_blocks, weighted, place_table)
        window = jnp.sum(window.reshape((parts, -1) + window.shape[1:]), axis=0)
        lower = window[:, :blocks_dev]
        middle = window[:, blocks_dev : 2 * blocks_dev]
        upper = window[:, 2 * blocks_dev :]
        got_odd, got_even = ring_pairs(jnp.where(odd, upper, lower), jnp.where(odd, lower, upper))
        return middle + got_odd + got_even

    def push_unrounded(channels):
        weighted = channels * row_inverse
        high = lax.reduce_precision(weighted, 8, 7)
        low = weighted - high
        parts = jnp.concatenate([high, low]).astype(jnp.bfloat16)
        return push(parts, 2)

    def push_rounded(mass):
        return push((mass * row_inverse).astype(jnp.bfloat16)[None])[0]

    raw_1 = 0.85 * push_rounded(start_mass.reshape(blocks_dev, tile_width)) + 0.15
    ones = jnp.ones_like(raw_1)
    chain_2, ones_1 = push_unrounded(jnp.stack([raw_1, ones]))
    chain_3, ones_2 = push_unrounded(jnp.stack([chain_2, ones_1]))
    (chain_4,) = push_unrounded(chain_3[None])
    wanted = (
        (raw_1, raw_1),
        (chain_2, chain_2), (chain_2, ones),
        (chain_3, chain_3), (chain_3, ones_1), (chain_3, ones), (ones_1, ones_1), (ones_1, ones),
        (chain_4, chain_4), (chain_4, ones_2), (chain_4, ones_1), (chain_4, ones),
        (ones_2, ones_2), (ones_2, ones_1), (ones_2, ones),
    )
    sums = all_sum(jnp.stack([jnp.sum(a * b) for a, b in wanted]))
    (r11, c22, c2o, c33, c3p, c3o, pp, po, c44, c4q, c4p, c4o, qq, qp, qo) = sums

    scale_1 = zone_root / jnp.sqrt(r11)
    a2 = 0.85 * scale_1
    scale_2 = zone_root / jnp.sqrt(a2 * a2 * c22 + 2.0 * 0.15 * a2 * c2o + 0.15 * 0.15 * zones)
    p3 = 0.85 * scale_2 * 0.15
    a3 = 0.85 * scale_2 * a2
    scale_3 = zone_root / jnp.sqrt(
        a3 * a3 * c33 + 2.0 * a3 * (p3 * c3p + 0.15 * c3o) + p3 * p3 * pp + 0.3 * p3 * po + 0.15 * 0.15 * zones
    )
    a4 = 0.85 * scale_3 * a3
    q4 = 0.85 * scale_3 * p3
    p4 = 0.85 * scale_3 * 0.15
    scale_4 = zone_root / jnp.sqrt(
        a4 * a4 * c44 + 2.0 * a4 * (q4 * c4q + p4 * c4p + 0.15 * c4o)
        + q4 * q4 * qq + p4 * p4 * pp + 2.0 * q4 * (p4 * qp + 0.15 * qo) + 0.3 * p4 * po + 0.15 * 0.15 * zones
    )
    raw_mass = raw_1
    for scale in (scale_1, scale_2, scale_3):
        raw_mass = 0.85 * push_rounded(raw_mass * scale) + 0.15
    stationary = raw_mass * scale_4

    root_mass = jnp.sqrt(stationary)
    probe_rows = probe_block.reshape(chans, blocks_dev, tile_width).astype(jnp.float32)
    probe_odd, probe_even = ring_pairs(probe_block, probe_block)
    root_odd, root_even = ring_pairs(root_mass, root_mass)

    def window_of(own, got_odd, got_even, dim):
        before = jnp.where(odd, got_even, got_odd)
        after = jnp.where(odd, got_odd, got_even)
        return jnp.concatenate([before, own, after], axis=dim)

    plain_window = window_of(probe_block, probe_odd, probe_even, 1)
    root_window = window_of(root_mass, root_odd, root_even, 0).reshape(-1)
    pushed = (probe_rows * (root_mass * row_inverse)[None]).astype(jnp.bfloat16)
    landed = push(pushed)
    probe_window = (plain_window.astype(jnp.float32) / root_window[None, :]).astype(jnp.bfloat16)
    probe_window = probe_window.reshape(chans, 3 * blocks_dev, tile_width)
    gathered = probe_window[:, local_index] * live_slots.astype(jnp.bfloat16)[None, :, :, None]
    forward_term = jnp.einsum("bkij,cbkj->cbi", tile_blocks, gathered, preferred_element_type=jnp.float32)
    forward_term = forward_term * (root_mass * row_inverse)[None]
    transposed_term = landed / root_mass[None]
    embedded = (0.5 * (forward_term + transposed_term)).reshape(chans, blocks_dev * tile_width)
    gram_matrix = all_sum(jnp.dot(embedded, embedded.T, precision=HIGHEST))
    lower_factor = jnp.linalg.cholesky(gram_matrix)
    return jax.scipy.linalg.solve_triangular(lower_factor, embedded, lower=True)


def solution(mesh):
    return jax.shard_map(
        per_device,
        mesh=mesh,
        in_specs=(P(RING, None, None, None), P(RING, None), P(RING), P(RING), P(None, RING)),
        out_specs=P(None, RING),
        check_vma=False,
    )
```

```python
import functools
import math

import jax
import jax.numpy as jnp
from jax import lax
from jax.experimental import pallas as pl
from jax.experimental.pallas import tpu as pltpu
from jax.sharding import PartitionSpec as P

RING = ("rows", "cols")
F32 = jnp.float32
BF16 = jnp.bfloat16
HIGHEST = lax.Precision.HIGHEST
LAST_DIMS = (((1,), (1,)), ((), ()))
SMEM = pl.BlockSpec(memory_space=pltpu.SMEM)
VMEM = pl.BlockSpec(memory_space=pltpu.VMEM)
ANY = pl.BlockSpec(memory_space=pl.ANY)


def swap(shard, axis, partner):
    count = lax.axis_size(axis)
    return lax.ppermute(shard, axis, [(i, partner(i) % count) for i in range(count)])


def ring_pairs(shard_odd, shard_even):
    got_odd = swap(shard_odd, RING, lambda i: i + 1 if i % 2 else i - 1)
    got_even = swap(shard_even, RING, lambda i: i - 1 if i % 2 else i + 1)
    return got_odd, got_even


def all_sum(part):
    part = part + swap(part, "rows", lambda i: i ^ 1)
    part = part + sum(swap(part, "cols", lambda i, d=d: i ^ d) for d in (2, 1, 3))
    part = part + sum(swap(part, "rows", lambda i, d=d: i ^ d) for d in (4, 2, 6))
    part = part + swap(part, "rows", lambda i: i ^ 8)
    return part + sum(
        swap(part, "rows", lambda i, d=d: i + 8 * d if (i // 8) % 2 else i - 8 * d) for d in (3, 2, 1)
    )


def push(target_ref, tiles_ref, parts, window, outs):
    blocks, slots = tiles_ref.shape[:2]
    height = parts[0].shape[0]
    window[...] = jnp.zeros_like(window)
    rows = jnp.concatenate(parts, axis=0) if len(parts) > 1 else parts[0]
    owner = lax.broadcasted_iota(jnp.int32, rows.shape, 0) % blocks
    for block in range(blocks):
        left = jnp.where(owner == block, rows, 0.0).astype(BF16)
        for slot in range(slots):
            product = jnp.dot(left, tiles_ref[block, slot], preferred_element_type=F32)
            if len(parts) > 1:
                product = product[:height] + product[height:]
            window[target_ref[block * slots + slot]] += product
    for channel in range(height // blocks):
        rows = slice(channel * blocks, (channel + 1) * blocks)
        landed = jnp.sum(window[0 : 3 * blocks, rows, :], axis=1)
        for part, out in zip((0, 1, 2), outs):
            out[rows, :] = landed[part * blocks : (part + 1) * blocks]


def two_parts(value):
    high = value.astype(BF16).astype(F32)
    return high, value - high


def load_kernel(target_ref, count_ref, tiles_hbm, start_ref, tiles_ref, inverse_ref, odd_ref, own_ref, even_ref, window, sems):
    blocks, slots, width = tiles_ref.shape[:3]
    copies = [pltpu.make_async_copy(tiles_hbm.at[b], tiles_ref.at[b], sems.at[b]) for b in range(blocks)]
    for copy in copies:
        copy.start()
    ones = jnp.ones((8, width), BF16)
    sums = []
    for block in range(blocks):
        copies[block].wait()
        total = jnp.zeros((8, width), F32)
        for slot in range(slots):
            part = lax.dot_general(ones, tiles_ref[block, slot], LAST_DIMS, preferred_element_type=F32)
            total = total + jnp.where(slot < count_ref[block], part, 0.0)
        sums.append(total[0:1])
    inverse = 1.0 / jnp.concatenate(sums, axis=0)
    inverse_ref[...] = inverse
    push(target_ref, tiles_ref, (start_ref[...] * inverse,), window, (odd_ref, own_ref, even_ref))


def second_kernel(target_ref, tiles_ref, inverse_ref, odd, own, even, to_odd, kept, to_even, value_ref, window):
    raw = 0.85 * (own[...] + odd[...] + even[...]) + 0.15
    value_ref[...] = raw
    inverse = inverse_ref[...]
    rows = jnp.concatenate([raw * inverse, inverse], axis=0)
    push(target_ref, tiles_ref, two_parts(rows), window, (to_odd, kept, to_even))


def chain_kernel(channels, target_ref, tiles_ref, inverse_ref, odd, own, even, to_odd, kept, to_even, value_ref, window):
    value = own[...] + odd[...] + even[...]
    value_ref[...] = value
    inverse = inverse_ref[...]
    rows = jnp.concatenate([value[8 * c : 8 * c + 8] * inverse for c in range(channels)], axis=0)
    push(target_ref, tiles_ref, two_parts(rows), window, (to_odd, kept, to_even))


def sums_kernel(raw_ref, second_ref, third_ref, odd, own, even, out_ref):
    raw = raw_ref[...]
    second = second_ref[0:8]
    ones_1 = second_ref[8:16]
    third = third_ref[0:8]
    ones_2 = third_ref[8:16]
    fourth = own[...] + odd[...] + even[...]
    wanted = (
        raw * raw,
        second * second, second,
        third * third, third * ones_1, third, ones_1 * ones_1, ones_1,
        fourth * fourth, fourth * ones_2, fourth * ones_1, fourth,
        ones_2 * ones_2, ones_2 * ones_1, ones_2, jnp.zeros_like(raw),
    )
    lines = [jnp.sum(term[:, :128] + term[:, 128:], axis=0, keepdims=True) for term in wanted]
    out_ref[...] = jnp.concatenate(lines, axis=0)


def scales_of(sums, zones):
    totals = jnp.sum(sums, axis=1, keepdims=True)
    (r11, c22, c2o, c33, c3p, c3o, pp, po, c44, c4q, c4p, c4o, qq, qp, qo) = (totals[i : i + 1] for i in range(15))
    root = math.sqrt(zones)
    floor = 0.15 * 0.15 * zones
    scale_1 = root / jnp.sqrt(r11)
    a2 = 0.85 * scale_1
    scale_2 = root / jnp.sqrt(a2 * a2 * c22 + 0.3 * a2 * c2o + floor)
    a3 = 0.85 * scale_2 * a2
    p3 = 0.85 * scale_2 * 0.15
    scale_3 = root / jnp.sqrt(
        a3 * a3 * c33 + 2.0 * a3 * (p3 * c3p + 0.15 * c3o) + p3 * p3 * pp + 0.3 * p3 * po + floor
    )
    a4 = 0.85 * scale_3 * a3
    q4 = 0.85 * scale_3 * p3
    p4 = 0.85 * scale_3 * 0.15
    scale_4 = root / jnp.sqrt(
        a4 * a4 * c44 + 2.0 * a4 * (q4 * c4q + p4 * c4p + 0.15 * c4o)
        + q4 * q4 * qq + p4 * p4 * pp + 2.0 * q4 * (p4 * qp + 0.15 * qo) + 0.3 * p4 * po + floor
    )
    return scale_1, scale_2, scale_3, scale_4


def replay_kernel(zones, target_ref, tiles_ref, inverse_ref, sums_ref, raw_ref, to_odd, kept, to_even, scales_ref, window):
    scales = scales_of(sums_ref[...], zones)
    for place, scale in enumerate(scales):
        scales_ref[place : place + 1, :] = jnp.broadcast_to(scale, (1, 128))
    rows = (raw_ref[...] * scales[0]) * inverse_ref[...]
    push(target_ref, tiles_ref, (rows,), window, (to_odd, kept, to_even))


def again_kernel(place, target_ref, tiles_ref, inverse_ref, scales_ref, odd, own, even, to_odd, kept, to_even, window):
    raw = 0.85 * (own[...] + odd[...] + even[...]) + 0.15
    rows = (raw * scales_ref[place : place + 1, 0:1]) * inverse_ref[...]
    push(target_ref, tiles_ref, (rows,), window, (to_odd, kept, to_even))


def transposed_kernel(target_ref, tiles_ref, inverse_ref, scales_ref, odd, own, even, probe_ref, to_odd, kept, to_even, root_ref, window):
    blocks, slots, width = tiles_ref.shape[:3]
    raw = 0.85 * (own[...] + odd[...] + even[...]) + 0.15
    root = jnp.sqrt(raw * scales_ref[3:4, 0:1])
    root_ref[...] = root
    gain = root * inverse_ref[...]
    window[...] = jnp.zeros_like(window)
    for block in range(blocks):
        probe = probe_ref[:, block * width : (block + 1) * width].astype(F32)
        left = (probe * gain[block : block + 1]).astype(BF16)
        for slot in range(slots):
            product = jnp.dot(left, tiles_ref[block, slot], preferred_element_type=F32)
            window[target_ref[block * slots + slot]] += product
    to_odd[...] = window[0:blocks]
    kept[...] = window[blocks : 2 * blocks]
    to_even[...] = window[2 * blocks : 3 * blocks]


def forward_kernel(target_ref, tiles_ref, inverse_ref, root_odd, root_own, root_even, probe_odd, probe_own, probe_even, out_ref, window):
    blocks, slots, width = tiles_ref.shape[:3]
    for part, (root_ref, probe_ref) in enumerate(((root_odd, probe_odd), (root_own, probe_own), (root_even, probe_even))):
        inverse_root = 1.0 / root_ref[...]
        for block in range(blocks):
            probe = probe_ref[:, block * width : (block + 1) * width].astype(F32)
            window[part * blocks + block] = (probe * inverse_root[block : block + 1]).astype(BF16)
    window[3 * blocks] = jnp.zeros(window.shape[1:], BF16)
    gain = root_own[...] * inverse_ref[...]
    for block in range(blocks):
        total = jnp.zeros(window.shape[1:], F32)
        for slot in range(slots):
            left = window[target_ref[block * slots + slot]]
            total += lax.dot_general(left, tiles_ref[block, slot], LAST_DIMS, preferred_element_type=F32)
        out_ref[block] = total * gain[block : block + 1]


def embed_kernel(forward_ref, odd, own, even, root_ref, out_ref, gram_ref):
    blocks, chans, width = forward_ref.shape
    inverse_root = 1.0 / root_ref[...]
    gram = jnp.zeros((chans, chans), F32)
    for block in range(blocks):
        landed = own[block] + odd[block] + even[block]
        embedded = 0.5 * (forward_ref[block] + landed * inverse_root[block : block + 1])
        out_ref[:, block * width : (block + 1) * width] = embedded
        gram += lax.dot_general(embedded, embedded, LAST_DIMS, precision=HIGHEST, preferred_element_type=F32)
    gram_ref[...] = gram


def basis_kernel(gram_ref, embedded_ref, out_ref):
    size = gram_ref.shape[0]
    row = lax.broadcasted_iota(jnp.int32, (size, size), 0)
    col = lax.broadcasted_iota(jnp.int32, (size, size), 1)
    identity = jnp.where(row == col, 1.0, 0.0)
    work = jnp.concatenate([gram_ref[...], identity], axis=1)
    line = lax.broadcasted_iota(jnp.int32, (size, 1), 0)
    for step in range(size):
        pivot_row = work[step : step + 1, :]
        factor = work[:, step : step + 1] * (1.0 / pivot_row[:, step : step + 1])
        work = work - jnp.where(line > step, factor, 0.0) * pivot_row
    pivots = jnp.sum(work[:, :size] * identity, axis=1, keepdims=True)
    inverse = work[:, size:] * (1.0 / jnp.sqrt(pivots))
    out_ref[...] = jnp.dot(inverse, embedded_ref[...], precision=HIGHEST, preferred_element_type=F32)


def call(kernel, name, outs, operands, specs, scratch, limit=24):
    return pl.pallas_call(
        kernel,
        out_shape=outs,
        in_specs=specs,
        out_specs=[VMEM] * len(outs),
        scratch_shapes=scratch,
        compiler_params=pltpu.CompilerParams(vmem_limit_bytes=limit << 20),
        name=name,
    )(*operands)


def per_device(tile_blocks, tile_cols, tile_count, start_mass, probe_block):
    blocks, slots, width = tile_blocks.shape[:3]
    chans = probe_block.shape[0]
    total_blocks = blocks * lax.axis_size(RING)
    zones = total_blocks * width
    place = lax.axis_index(RING)
    live = jnp.arange(slots)[None, :] < tile_count[:, None]
    place_in_window = (tile_cols - place * blocks + blocks) % total_blocks
    before = place_in_window < blocks
    after = place_in_window >= 2 * blocks
    flipped = jnp.where(before, place_in_window + 2 * blocks, jnp.where(after, place_in_window - 2 * blocks, place_in_window))
    target = jnp.where(place % 2 == 1, flipped, place_in_window)
    target = jnp.where(live, target, 3 * blocks).reshape(-1).astype(jnp.int32)

    def rows(channels=1):
        return jax.ShapeDtypeStruct((channels * blocks, width), F32)

    def window(channels, kind=F32):
        return pltpu.VMEM((3 * blocks + 1, channels, width), kind)

    tiles, inverse, to_odd, own, to_even = call(
        load_kernel, "load",
        [pltpu.VMEM(tile_blocks.shape, BF16), rows(), rows(), rows(), rows()],
        (target, tile_count, tile_blocks, start_mass.reshape(blocks, width)),
        [SMEM, SMEM, ANY, VMEM],
        [window(blocks), pltpu.SemaphoreType.DMA((blocks,))],
    )
    tiles = pltpu.with_memory_space_constraint(tiles, pltpu.VMEM)
    odd, even = ring_pairs(to_odd, to_even)

    def step(kernel, name, channels_out, operands, extra, scratch=None):
        specs = [SMEM] + [VMEM] * (2 + len(operands))
        outs = [rows(channels_out)] * 3 + extra
        scratch = [window(channels_out * blocks)] if scratch is None else scratch
        return call(kernel, name, outs, (target, tiles, inverse, *operands), specs, scratch)

    to_odd, own, to_even, raw = step(second_kernel, "second", 2, (odd, own, even), [rows()])
    odd, even = ring_pairs(to_odd, to_even)
    to_odd, own, to_even, second = step(functools.partial(chain_kernel, 2), "third", 2, (odd, own, even), [rows(2)])
    odd, even = ring_pairs(to_odd, to_even)
    to_odd, own, to_even, third = step(functools.partial(chain_kernel, 1), "fourth", 1, (odd, own, even), [rows(2)])
    odd, even = ring_pairs(to_odd, to_even)
    (sums,) = call(
        sums_kernel, "sums", [jax.ShapeDtypeStruct((16, 128), F32)], (raw, second, third, odd, own, even), [VMEM] * 6, []
    )
    sums = all_sum(sums)
    to_odd, own, to_even, scales = step(
        functools.partial(replay_kernel, zones), "replay_2", 1, (sums, raw), [jax.ShapeDtypeStruct((8, 128), F32)]
    )
    odd, even = ring_pairs(to_odd, to_even)
    to_odd, own, to_even = step(functools.partial(again_kernel, 1), "replay_3", 1, (scales, odd, own, even), [])
    odd, even = ring_pairs(to_odd, to_even)
    to_odd, own, to_even = step(functools.partial(again_kernel, 2), "replay_4", 1, (scales, odd, own, even), [])
    odd, even = ring_pairs(to_odd, to_even)

    wide = jax.ShapeDtypeStruct((blocks, chans, width), F32)
    probe_odd, probe_even = ring_pairs(probe_block, probe_block)
    to_odd, own, to_even, root = call(
        transposed_kernel, "transposed", [wide, wide, wide, rows()],
        (target, tiles, inverse, scales, odd, own, even, probe_block),
        [SMEM] + [VMEM] * 7, [window(chans)],
    )
    root_odd, root_even = ring_pairs(root, root)
    odd, even = ring_pairs(to_odd, to_even)
    (forward,) = call(
        forward_kernel, "forward", [wide],
        (target, tiles, inverse, root_odd, root, root_even, probe_odd, probe_block, probe_even),
        [SMEM] + [VMEM] * 8, [window(chans, BF16)],
    )
    embedded, gram = call(
        embed_kernel, "embed",
        [jax.ShapeDtypeStruct((chans, blocks * width), F32), jax.ShapeDtypeStruct((chans, chans), F32)],
        (forward, odd, own, even, root), [VMEM] * 5, [],
    )
    gram = all_sum(gram)
    (basis,) = call(
        basis_kernel, "basis", [jax.ShapeDtypeStruct((chans, blocks * width), F32)], (gram, embedded), [VMEM] * 2, []
    )
    return basis


def solution(mesh):
    return jax.shard_map(
        per_device,
        mesh=mesh,
        in_specs=(P(RING, None, None, None), P(RING, None), P(RING), P(RING), P(None, RING)),
        out_specs=P(None, RING),
        check_vma=False,
    )
```

```python
import functools
import math

import jax
import jax.numpy as jnp
from jax import lax
from jax.experimental import pallas as pl
from jax.experimental.pallas import tpu as pltpu
from jax.sharding import PartitionSpec as P

RING = ("rows", "cols")
F32 = jnp.float32
BF16 = jnp.bfloat16
HIGHEST = lax.Precision.HIGHEST
LAST_DIMS = (((1,), (1,)), ((), ()))
SMEM = pl.BlockSpec(memory_space=pltpu.SMEM)
VMEM = pl.BlockSpec(memory_space=pltpu.VMEM)
CHUNK = 8
DEAD = 24
HALO_CHUNKS = 128
OWN_CHUNKS = 129
SPARE = 130


def swap(shard, axis, partner):
    count = lax.axis_size(axis)
    return lax.ppermute(shard, axis, [(i, partner(i) % count) for i in range(count)])


def ring_pairs(shard_odd, shard_even):
    got_odd = swap(shard_odd, RING, lambda i: i + 1 if i % 2 else i - 1)
    got_even = swap(shard_even, RING, lambda i: i - 1 if i % 2 else i + 1)
    return got_odd, got_even


def gathered(part, axis, groups):
    spread = jnp.broadcast_to(part[None], (len(groups[0]), *part.shape))
    return lax.all_to_all(spread, axis, 0, 0, tiled=True, axis_index_groups=groups)


def chip_parts(part):
    part = part + swap(part, "rows", lambda i: i ^ 1)
    cols = lax.axis_size("cols")
    devices = lax.axis_size(RING)
    groups = [[i for i in range(devices) if (i // cols) % 2 == core] for core in (0, 1)]
    return gathered(part, RING, groups)


def plane_parts(part):
    part = part + swap(part, "rows", lambda i: i ^ 1)
    part = part + sum(swap(part, "cols", lambda i, d=d: i ^ d) for d in (2, 1, 3))
    groups = [list(range(core, lax.axis_size("rows"), 2)) for core in (0, 1)]
    return gathered(part, "rows", groups)


def two_parts(value):
    high = value.astype(BF16).astype(F32)
    return high, value - high


def spread_blocks(rows, left_ref):
    blocks, height = left_ref.shape[:2]
    if rows.shape[0] < height:
        rows = jnp.concatenate([rows, jnp.zeros((height - rows.shape[0], rows.shape[1]), F32)], axis=0)
    owner = lax.broadcasted_iota(jnp.int32, rows.shape, 0) % blocks
    for block in range(blocks):
        left_ref[block] = jnp.where(owner == block, rows, 0.0).astype(BF16)


def for_tiles(table_ref, own, visit):
    first = 64 if own else 0

    def chunk(number, carry):
        for place in range(CHUNK):
            entry = table_ref[first + number * CHUNK + place]
            visit(entry >> 5, entry & 31)
        return carry

    lax.fori_loop(0, table_ref[OWN_CHUNKS if own else HALO_CHUNKS], chunk, 0)


def push_rows(table_ref, own, tiles_ref, left_ref, window, split):
    height = window.shape[1]
    window[...] = jnp.zeros_like(window)

    def visit(tile, target):
        product = jnp.dot(left_ref[tile >> 3], tiles_ref[tile], preferred_element_type=F32)
        if split:
            product = product[:height] + product[height : 2 * height]
        window[target] += product[:height]

    for_tiles(table_ref, own, visit)


def landed(window, part, out):
    for channel in range(out.shape[0] // 8):
        rows = slice(channel * 8, (channel + 1) * 8)
        out[rows, :] = jnp.sum(window[part * 8 : (part + 1) * 8, rows, :], axis=1)


def load_kernel(cols_hbm, count_hbm, tiles_hbm, start_hbm, tiles_ref, target_ref, inverse_ref, odd_ref, own_ref, even_ref,
                window, start_ref, cols_ref, count_ref, sems, small_sems):
    blocks, slots, width = tiles_hbm.shape[:3]
    small = [
        pltpu.make_async_copy(cols_hbm, cols_ref, small_sems.at[0]),
        pltpu.make_async_copy(count_hbm, count_ref, small_sems.at[1]),
    ]
    small += [
        pltpu.make_async_copy(start_hbm.at[pl.ds(b * width, width)], start_ref.at[b], small_sems.at[2 + b]) for b in range(blocks)
    ]
    copies = [
        pltpu.make_async_copy(tiles_hbm.at[b], tiles_ref.at[pl.ds(b * slots, slots)], sems.at[b]) for b in range(blocks)
    ]
    for copy in small + copies:
        copy.start()
    ones = jnp.ones((16, 128), BF16)
    window[...] = jnp.zeros_like(window)
    line = lax.broadcasted_iota(jnp.int32, (16, width), 0)
    total_blocks = blocks * lax.axis_size("rows") * lax.axis_size("cols")
    place = lax.axis_index("rows") * lax.axis_size("cols") + lax.axis_index("cols")
    swapped = place % 2 == 1
    for copy in small:
        copy.wait()

    def row_sums(block):
        folded = jnp.zeros((width, 128), F32)
        for slot in range(slots):
            tile = tiles_ref[block * slots + slot].astype(F32)
            folded = folded + (tile[:, :128] + tile[:, 128:]) * jnp.where(slot < count_ref[block], 1.0, 0.0)
        total = jnp.zeros((16, width), F32)
        for _ in range(3):
            part = folded.astype(BF16)
            folded = folded - part.astype(F32)
            total = total + lax.dot_general(ones, part, LAST_DIMS, preferred_element_type=F32)
        return total

    def target_of(block, slot):
        target = cols_ref[block, slot] - place * blocks + blocks
        target = jnp.where(target < 0, target + total_blocks, target)
        target = jnp.where(target >= total_blocks, target - total_blocks, target)
        flipped = jnp.where(target >= 2 * blocks, target - 2 * blocks, jnp.where(target < blocks, target + 2 * blocks, target))
        target = jnp.where(swapped, flipped, target)
        return jnp.where(slot < count_ref[block], target, DEAD)

    def push_block(block, total):
        inverse = 1.0 / total
        inverse_ref[block : block + 1, :] = inverse[0:1]
        left = jnp.where(line == block, start_ref[block : block + 1, :] * inverse, 0.0).astype(BF16)
        for slot in range(slots):
            tile = block * slots + slot
            target = target_of(block, slot)
            target_ref[tile] = target
            window[target] += jnp.dot(left, tiles_ref[tile], preferred_element_type=F32)[0:8]

    before = None
    for block in range(blocks):
        copies[block].wait()
        total = row_sums(block)
        if before is not None:
            push_block(block - 1, before)
        before = total
    push_block(blocks - 1, before)
    landed(window, 0, odd_ref)
    landed(window, 1, own_ref)
    landed(window, 2, even_ref)


def table_kernel(target_ref, table_ref):
    for entry in range(128):
        table_ref[entry] = DEAD
    halo_count, own_count = jnp.int32(0), jnp.int32(0)
    for tile in range(target_ref.shape[0]):
        target = target_ref[tile]
        to_own = (target >= 8) & (target < 16)
        to_halo = (target < 8) | ((target >= 16) & (target < DEAD))
        entry = target + tile * 32
        table_ref[jnp.where(to_halo, halo_count, jnp.where(to_own, 64 + own_count, SPARE))] = entry
        halo_count += jnp.where(to_halo, 1, 0)
        own_count += jnp.where(to_own, 1, 0)
    table_ref[HALO_CHUNKS] = (halo_count + CHUNK - 1) >> 3
    table_ref[OWN_CHUNKS] = (own_count + CHUNK - 1) >> 3


def halo_step(rows, split, table_ref, tiles_ref, to_odd, to_even, left_ref, window):
    spread_blocks(jnp.concatenate(two_parts(rows), axis=0) if split else rows, left_ref)
    push_rows(table_ref, False, tiles_ref, left_ref, window, split)
    landed(window, 0, to_odd)
    landed(window, 2, to_even)


def second_kernel(table_ref, tiles_ref, inverse_ref, odd, own, even, to_odd, to_even, left_ref, value_ref, window):
    raw = 0.85 * (own[...] + odd[...] + even[...]) + 0.15
    value_ref[...] = raw
    inverse = inverse_ref[...]
    rows = jnp.concatenate([raw * inverse, inverse], axis=0)
    halo_step(rows, True, table_ref, tiles_ref, to_odd, to_even, left_ref, window)


def chain_kernel(channels, table_ref, tiles_ref, inverse_ref, odd, own, even, to_odd, to_even, left_ref, value_ref, window):
    value = own[...] + odd[...] + even[...]
    value_ref[...] = value
    inverse = inverse_ref[...]
    rows = [value[8 * c : 8 * c + 8] * inverse for c in range(channels)]
    rows = jnp.concatenate(rows, axis=0) if channels > 1 else rows[0]
    halo_step(rows, True, table_ref, tiles_ref, to_odd, to_even, left_ref, window)


def own_kernel(split, table_ref, tiles_ref, left_ref, kept, window):
    push_rows(table_ref, True, tiles_ref, left_ref, window, split)
    landed(window, 1, kept)


def sums_kernel(raw_ref, second_ref, third_ref, odd, own, even, out_ref):
    raw = raw_ref[...]
    second = second_ref[0:8]
    ones_1 = second_ref[8:16]
    third = third_ref[0:8]
    ones_2 = third_ref[8:16]
    fourth = own[...] + odd[...] + even[...]
    wanted = (
        raw * raw,
        second * second, second,
        third * third, third * ones_1, third, ones_1 * ones_1, ones_1,
        fourth * fourth, fourth * ones_2, fourth * ones_1, fourth,
        ones_2 * ones_2, ones_2 * ones_1, ones_2, jnp.zeros_like(raw),
    )
    lines = [jnp.sum(term[:, :128] + term[:, 128:], axis=0, keepdims=True) for term in wanted]
    lines = jnp.sum(jnp.concatenate(lines, axis=0), axis=1, keepdims=True)
    row = lax.broadcasted_iota(jnp.int32, (16, 128), 0)
    lane = lax.broadcasted_iota(jnp.int32, (16, 128), 1)
    out_ref[...] = jnp.sum(jnp.where(row == lane, lines, 0.0), axis=0, keepdims=True)


def scales_of(sums, zones):
    line = jnp.broadcast_to(jnp.sum(sums, axis=0, keepdims=True), (16, 128))
    row = lax.broadcasted_iota(jnp.int32, line.shape, 0)
    lane = lax.broadcasted_iota(jnp.int32, line.shape, 1)
    totals = jnp.sum(jnp.where(row == lane, line, 0.0), axis=1, keepdims=True)
    (r11, c22, c2o, c33, c3p, c3o, pp, po, c44, c4q, c4p, c4o, qq, qp, qo) = (totals[i : i + 1] for i in range(15))
    root = math.sqrt(zones)
    floor = 0.15 * 0.15 * zones
    scale_1 = root / jnp.sqrt(r11)
    a2 = 0.85 * scale_1
    scale_2 = root / jnp.sqrt(a2 * a2 * c22 + 0.3 * a2 * c2o + floor)
    a3 = 0.85 * scale_2 * a2
    p3 = 0.85 * scale_2 * 0.15
    scale_3 = root / jnp.sqrt(
        a3 * a3 * c33 + 2.0 * a3 * (p3 * c3p + 0.15 * c3o) + p3 * p3 * pp + 0.3 * p3 * po + floor
    )
    a4 = 0.85 * scale_3 * a3
    q4 = 0.85 * scale_3 * p3
    p4 = 0.85 * scale_3 * 0.15
    scale_4 = root / jnp.sqrt(
        a4 * a4 * c44 + 2.0 * a4 * (q4 * c4q + p4 * c4p + 0.15 * c4o)
        + q4 * q4 * qq + p4 * p4 * pp + 2.0 * q4 * (p4 * qp + 0.15 * qo) + 0.3 * p4 * po + floor
    )
    return scale_1, scale_2, scale_3, scale_4


def replay_kernel(zones, table_ref, tiles_ref, inverse_ref, sums_ref, raw_ref, to_odd, to_even, left_ref, scales_ref, window):
    scales = scales_of(sums_ref[...], zones)
    for place, scale in enumerate(scales):
        scales_ref[place : place + 1, :] = jnp.broadcast_to(scale, (1, 128))
    rows = (raw_ref[...] * scales[0]) * inverse_ref[...]
    halo_step(rows, False, table_ref, tiles_ref, to_odd, to_even, left_ref, window)


def again_kernel(place, table_ref, tiles_ref, inverse_ref, scales_ref, odd, own, even, to_odd, to_even, left_ref, window):
    raw = 0.85 * (own[...] + odd[...] + even[...]) + 0.15
    rows = (raw * scales_ref[place : place + 1, 0:1]) * inverse_ref[...]
    halo_step(rows, False, table_ref, tiles_ref, to_odd, to_even, left_ref, window)


def transposed_kernel(table_ref, tiles_ref, inverse_ref, scales_ref, odd, own, even, probe_ref, to_odd, to_even, pushed_ref, scaled_ref, root_ref, window):
    blocks, chans, width = pushed_ref.shape
    raw = 0.85 * (own[...] + odd[...] + even[...]) + 0.15
    root = jnp.sqrt(raw * scales_ref[3:4, 0:1])
    root_ref[...] = root
    inverse_root = 1.0 / root
    gain = root * inverse_ref[...]
    for block in range(blocks):
        probe = probe_ref[:, block * width : (block + 1) * width].astype(F32)
        pushed_ref[block] = (probe * gain[block : block + 1]).astype(BF16)
        scaled = (probe * inverse_root[block : block + 1]).astype(BF16)
        scaled_ref[block] = scaled
        to_odd[2 * blocks + block] = scaled
        to_even[2 * blocks + block] = scaled
    window[...] = jnp.zeros_like(window)

    def visit(tile, target):
        window[target] += jnp.dot(pushed_ref[tile >> 3], tiles_ref[tile], preferred_element_type=F32)

    for_tiles(table_ref, False, visit)
    for part, out in ((0, to_odd), (2, to_even)):
        for block in range(blocks):
            high, low = two_parts(window[part * blocks + block])
            out[block] = high.astype(BF16)
            out[blocks + block] = low.astype(BF16)


def own_products_kernel(table_ref, tiles_ref, pushed_ref, scaled_ref, kept, forward_ref, window, forward):
    blocks = pushed_ref.shape[0]
    window[...] = jnp.zeros_like(window)
    forward[...] = jnp.zeros_like(forward)

    def visit(tile, target):
        block = tile >> 3
        dead = target == DEAD
        place = jnp.where(dead, blocks, target - blocks)
        matrix = tiles_ref[tile]
        window[place] += jnp.dot(pushed_ref[block], matrix, preferred_element_type=F32)
        left = scaled_ref[jnp.where(dead, 0, place)]
        forward[jnp.where(dead, blocks, block)] += lax.dot_general(left, matrix, LAST_DIMS, preferred_element_type=F32)

    for_tiles(table_ref, True, visit)
    kept[...] = window[0:blocks]
    forward_ref[...] = forward[0:blocks]


def embed_kernel(table_ref, tiles_ref, inverse_ref, root_ref, kept, forward_ref, odd, even, out_ref, gram_ref, forward):
    blocks, chans, width = forward_ref.shape
    forward[0:blocks] = forward_ref[...]
    forward[blocks] = jnp.zeros((chans, width), F32)

    def visit(tile, target):
        dead = target == DEAD
        from_odd = odd[jnp.where(target < blocks, 2 * blocks + target, 2 * blocks)]
        from_even = even[jnp.where((target >= 2 * blocks) & (target < 3 * blocks), target, 2 * blocks)]
        left = jnp.where(target < blocks, from_odd, from_even)
        place = jnp.where(dead, blocks, tile >> 3)
        forward[place] += lax.dot_general(left, tiles_ref[tile], LAST_DIMS, preferred_element_type=F32)

    for_tiles(table_ref, False, visit)
    root = root_ref[...]
    inverse_root = 1.0 / root
    gain = root * inverse_ref[...]
    gram = jnp.zeros((chans, chans), F32)
    for block in range(blocks):
        landing = kept[block]
        for message in (odd, even):
            landing = landing + (message[block].astype(F32) + message[blocks + block].astype(F32))
        embedded = 0.5 * (forward[block] * gain[block : block + 1] + landing * inverse_root[block : block + 1])
        out_ref[:, block * width : (block + 1) * width] = embedded
        gram += lax.dot_general(embedded, embedded, LAST_DIMS, precision=HIGHEST, preferred_element_type=F32)
    gram_ref[...] = jnp.concatenate([gram[8 * i : 8 * i + 8] for i in range(4)], axis=1)


def basis_kernel(gram_ref, embedded_ref, out_ref):
    size = embedded_ref.shape[0]
    row = lax.broadcasted_iota(jnp.int32, (size, size), 0)
    col = lax.broadcasted_iota(jnp.int32, (size, size), 1)
    identity = jnp.where(row == col, 1.0, 0.0)
    gram = jnp.sum(gram_ref[...], axis=0)
    gram = jnp.concatenate([gram[:, size * i : size * (i + 1)] for i in range(4)], axis=0)
    work = jnp.concatenate([gram, identity, jnp.zeros((size, 128 - 2 * size), F32)], axis=1)
    line = lax.broadcasted_iota(jnp.int32, work.shape, 0)
    for first in range(0, size, 4):
        columns = [jnp.broadcast_to(work[:, first + i : first + i + 1], work.shape) for i in range(4)]
        for i in range(4):
            step = first + i
            factor = jnp.where(line > step, columns[i] * (1.0 / columns[i][step : step + 1, :]), 0.0)
            work = work - factor * work[step : step + 1, :]
            for j in range(i + 1, 4):
                columns[j] = columns[j] - factor * columns[j][step : step + 1, :]
    pivots = jnp.sum(work[:, :size] * identity, axis=1, keepdims=True)
    inverse = work[:, size : 2 * size] * (1.0 / jnp.sqrt(pivots))
    out_ref[...] = jnp.dot(inverse, embedded_ref[...], precision=HIGHEST, preferred_element_type=F32)


def call(kernel, name, outs, operands, specs, scratch, out_specs=None, limit=24, flops=0, moved=0):
    return pl.pallas_call(
        kernel,
        out_shape=outs,
        in_specs=specs,
        out_specs=out_specs or [VMEM] * len(outs),
        scratch_shapes=scratch,
        compiler_params=pltpu.CompilerParams(vmem_limit_bytes=limit << 20),
        cost_estimate=pl.CostEstimate(flops=flops, bytes_accessed=moved, transcendentals=0),
        name=name,
    )(*operands)


def per_device(tile_blocks, tile_cols, tile_count, start_mass, probe_block):
    blocks, slots, width = tile_blocks.shape[:3]
    chans = probe_block.shape[0]
    zones = blocks * lax.axis_size(RING) * width

    def rows(channels=1):
        return jax.ShapeDtypeStruct((channels * blocks, width), F32)

    def window(channels, kind=F32, places=3 * blocks + 1):
        return pltpu.VMEM((places, channels, width), kind)

    tiles, target, inverse, to_odd, own, to_even = call(
        load_kernel, "load",
        [pltpu.VMEM((blocks * slots, width, width), BF16), pltpu.SMEM((blocks * slots,), jnp.int32), rows(), rows(), rows(), rows()],
        [pltpu.with_memory_space_constraint(x, pltpu.HBM) for x in (tile_cols, tile_count, tile_blocks, start_mass)],
        [pl.BlockSpec(memory_space=pltpu.HBM)] * 4,
        [
            window(blocks), pltpu.VMEM((blocks, width), F32), pltpu.SMEM(tile_cols.shape, jnp.int32),
            pltpu.SMEM(tile_count.shape, jnp.int32), pltpu.SemaphoreType.DMA((blocks,)), pltpu.SemaphoreType.DMA((2 + blocks,)),
        ],
        [VMEM, SMEM, VMEM, VMEM, VMEM, VMEM],
    )
    tiles = pltpu.with_memory_space_constraint(tiles, pltpu.VMEM)
    odd, even = ring_pairs(to_odd, to_even)
    (table,) = call(
        table_kernel, "table", [pltpu.SMEM((136,), jnp.int32)], [pltpu.with_memory_space_constraint(target, pltpu.SMEM)], [SMEM], [],
        [SMEM], flops=1 << 25, moved=1 << 22,
    )
    table = pltpu.with_memory_space_constraint(table, pltpu.SMEM)

    def step(kernel, name, channels, split, operands, extra):
        height = max(16, channels * blocks * (2 if split else 1))
        left = jax.ShapeDtypeStruct((blocks, height, width), BF16)
        to_odd, to_even, left, *extra = call(
            kernel, name, [rows(channels)] * 2 + [left] + extra, (table, tiles, inverse, *operands),
            [SMEM] + [VMEM] * (2 + len(operands)), [window(channels * blocks)], flops=1 << 24, moved=1 << 21,
        )
        odd, even = ring_pairs(to_odd, to_even)
        (own,) = call(
            functools.partial(own_kernel, split), name + "_own", [rows(channels)], (table, tiles, left), [SMEM] + [VMEM] * 2,
            [window(channels * blocks)], flops=1 << 25, moved=1 << 22,
        )
        return odd, own, even, *extra

    odd, own, even, raw = step(second_kernel, "second", 2, True, (odd, own, even), [rows()])
    odd, own, even, second = step(functools.partial(chain_kernel, 2), "third", 2, True, (odd, own, even), [rows(2)])
    odd, own, even, third = step(functools.partial(chain_kernel, 1), "fourth", 1, True, (odd, own, even), [rows(2)])
    (sums,) = call(
        sums_kernel, "sums", [jax.ShapeDtypeStruct((1, 128), F32)], (raw, second, third, odd, own, even), [VMEM] * 6, []
    )
    sums = chip_parts(sums[0])
    odd, own, even, scales = step(
        functools.partial(replay_kernel, zones), "replay_2", 1, False, (sums, raw), [jax.ShapeDtypeStruct((8, 128), F32)]
    )
    odd, own, even = step(functools.partial(again_kernel, 1), "replay_3", 1, False, (scales, odd, own, even), [])
    odd, own, even = step(functools.partial(again_kernel, 2), "replay_4", 1, False, (scales, odd, own, even), [])

    message = jax.ShapeDtypeStruct((3 * blocks, chans, width), BF16)
    narrow = jax.ShapeDtypeStruct((blocks, chans, width), BF16)
    wide = jax.ShapeDtypeStruct((blocks, chans, width), F32)
    to_odd, to_even, pushed, scaled, root = call(
        transposed_kernel, "transposed", [message, message, narrow, narrow, rows()],
        (table, tiles, inverse, scales, odd, own, even, probe_block), [SMEM] + [VMEM] * 7, [window(chans)],
    )
    odd, even = ring_pairs(to_odd, to_even)
    kept, forward = call(
        own_products_kernel, "own_products", [wide, wide], (table, tiles, pushed, scaled), [SMEM] + [VMEM] * 3,
        [window(chans, places=blocks + 1)] * 2, flops=1 << 28, moved=1 << 23,
    )
    embedded, gram = call(
        embed_kernel, "embed",
        [jax.ShapeDtypeStruct((chans, blocks * width), F32), jax.ShapeDtypeStruct((8, 128), F32)],
        (table, tiles, inverse, root, kept, forward, odd, even), [SMEM] + [VMEM] * 7, [window(chans, places=blocks + 1)],
    )
    (basis,) = call(
        basis_kernel, "basis", [jax.ShapeDtypeStruct((chans, blocks * width), F32)], (plane_parts(gram), embedded), [VMEM] * 2, []
    )
    return basis


def solution(mesh):
    return jax.shard_map(
        per_device,
        mesh=mesh,
        in_specs=(P(RING, None, None, None), P(RING, None), P(RING), P(RING), P(None, RING)),
        out_specs=P(None, RING),
        check_vma=False,
    )
```

```python
import functools
import math

import jax
import jax.numpy as jnp
from jax import lax
from jax.experimental import pallas as pl
from jax.experimental.pallas import tpu as pltpu
from jax.sharding import PartitionSpec as P

RING = ("rows", "cols")
F32 = jnp.float32
BF16 = jnp.bfloat16
HIGHEST = lax.Precision.HIGHEST
LAST_DIMS = (((1,), (1,)), ((), ()))
SMEM = pl.BlockSpec(memory_space=pltpu.SMEM)
VMEM = pl.BlockSpec(memory_space=pltpu.VMEM)
CHUNK = 8
DEAD = 24
HALO_CHUNKS = 128
OWN_CHUNKS = 129
SPARE = 130


def swap(shard, axis, partner):
    count = lax.axis_size(axis)
    return lax.ppermute(shard, axis, [(i, partner(i) % count) for i in range(count)])


def ring_pairs(shard_odd, shard_even):
    got_odd = swap(shard_odd, RING, lambda i: i + 1 if i % 2 else i - 1)
    got_even = swap(shard_even, RING, lambda i: i - 1 if i % 2 else i + 1)
    return got_odd, got_even


def gathered(part, axis, groups):
    spread = jnp.broadcast_to(part[None], (len(groups[0]), *part.shape))
    return lax.all_to_all(spread, axis, 0, 0, tiled=True, axis_index_groups=groups)


def chip_parts(part):
    part = part + swap(part, "rows", lambda i: i ^ 1)
    cols = lax.axis_size("cols")
    devices = lax.axis_size(RING)
    groups = [[i for i in range(devices) if (i // cols) % 2 == core] for core in (0, 1)]
    return gathered(part, RING, groups)


def plane_parts(part):
    part = part + swap(part, "rows", lambda i: i ^ 1)
    part = part + sum(swap(part, "cols", lambda i, d=d: i ^ d) for d in (2, 1, 3))
    groups = [list(range(core, lax.axis_size("rows"), 2)) for core in (0, 1)]
    return gathered(part, "rows", groups)


def two_parts(value):
    high = value.astype(BF16).astype(F32)
    return high, value - high


def spread_blocks(rows, left_ref):
    blocks, height = left_ref.shape[:2]
    if rows.shape[0] < height:
        rows = jnp.concatenate([rows, jnp.zeros((height - rows.shape[0], rows.shape[1]), F32)], axis=0)
    owner = lax.broadcasted_iota(jnp.int32, rows.shape, 0) % blocks
    for block in range(blocks):
        left_ref[block] = jnp.where(owner == block, rows, 0.0).astype(BF16)


def for_tiles(table_ref, own, visit):
    first = 64 if own else 0

    def chunk(number, carry):
        for place in range(CHUNK):
            entry = table_ref[first + number * CHUNK + place]
            visit(entry >> 5, entry & 31)
        return carry

    lax.fori_loop(0, table_ref[OWN_CHUNKS if own else HALO_CHUNKS], chunk, 0)


def push_rows(table_ref, own, tiles_ref, left_ref, window, split):
    height = window.shape[1]
    window[...] = jnp.zeros_like(window)

    def visit(tile, target):
        product = jnp.dot(left_ref[tile >> 3], tiles_ref[tile], preferred_element_type=F32)
        if split:
            product = product[:height] + product[height : 2 * height]
        window[target] += product[:height]

    for_tiles(table_ref, own, visit)


def landed(window, part, out):
    for channel in range(out.shape[0] // 8):
        rows = slice(channel * 8, (channel + 1) * 8)
        out[rows, :] = jnp.sum(window[part * 8 : (part + 1) * 8, rows, :], axis=1)


def load_kernel(cols_hbm, count_hbm, tiles_hbm, start_hbm, tiles_ref, target_ref, inverse_ref, odd_ref, own_ref, even_ref,
                window, start_ref, cols_ref, count_ref, sems, small_sems):
    blocks, slots, width = tiles_hbm.shape[:3]
    small = [
        pltpu.make_async_copy(cols_hbm, cols_ref, small_sems.at[0]),
        pltpu.make_async_copy(count_hbm, count_ref, small_sems.at[1]),
    ]
    small += [
        pltpu.make_async_copy(start_hbm.at[pl.ds(b * width, width)], start_ref.at[b], small_sems.at[2 + b]) for b in range(blocks)
    ]
    copies = [
        pltpu.make_async_copy(tiles_hbm.at[b], tiles_ref.at[pl.ds(b * slots, slots)], sems.at[b]) for b in range(blocks)
    ]
    for copy in small + copies:
        copy.start()
    ones = jnp.ones((16, 128), BF16)
    window[...] = jnp.zeros_like(window)
    line = lax.broadcasted_iota(jnp.int32, (16, width), 0)
    total_blocks = blocks * lax.axis_size("rows") * lax.axis_size("cols")
    place = lax.axis_index("rows") * lax.axis_size("cols") + lax.axis_index("cols")
    swapped = place % 2 == 1
    for copy in small:
        copy.wait()

    def row_sums(block):
        folded = jnp.zeros((width, 128), F32)
        for slot in range(slots):
            tile = tiles_ref[block * slots + slot].astype(F32)
            folded = folded + (tile[:, :128] + tile[:, 128:]) * jnp.where(slot < count_ref[block], 1.0, 0.0)
        total = jnp.zeros((16, width), F32)
        for _ in range(3):
            part = folded.astype(BF16)
            folded = folded - part.astype(F32)
            total = total + lax.dot_general(ones, part, LAST_DIMS, preferred_element_type=F32)
        return total

    def target_of(block, slot):
        target = cols_ref[block, slot] - place * blocks + blocks
        target = jnp.where(target < 0, target + total_blocks, target)
        target = jnp.where(target >= total_blocks, target - total_blocks, target)
        flipped = jnp.where(target >= 2 * blocks, target - 2 * blocks, jnp.where(target < blocks, target + 2 * blocks, target))
        target = jnp.where(swapped, flipped, target)
        return jnp.where(slot < count_ref[block], target, DEAD)

    def push_block(block, total):
        inverse = 1.0 / total
        inverse_ref[block : block + 1, :] = inverse[0:1]
        left = jnp.where(line == block, start_ref[block : block + 1, :] * inverse, 0.0).astype(BF16)
        for slot in range(slots):
            tile = block * slots + slot
            target = target_of(block, slot)
            target_ref[tile] = target
            window[target] += jnp.dot(left, tiles_ref[tile], preferred_element_type=F32)[0:8]

    before = None
    for block in range(blocks):
        copies[block].wait()
        total = row_sums(block)
        if before is not None:
            push_block(block - 1, before)
        before = total
    push_block(blocks - 1, before)
    landed(window, 0, odd_ref)
    landed(window, 1, own_ref)
    landed(window, 2, even_ref)


def table_kernel(target_ref, table_ref):
    for entry in range(128):
        table_ref[entry] = DEAD
    halo_count, own_count = jnp.int32(0), jnp.int32(0)
    for tile in range(target_ref.shape[0]):
        target = target_ref[tile]
        to_own = (target >= 8) & (target < 16)
        to_halo = (target < 8) | ((target >= 16) & (target < DEAD))
        entry = target + tile * 32
        table_ref[jnp.where(to_halo, halo_count, jnp.where(to_own, 64 + own_count, SPARE))] = entry
        halo_count += jnp.where(to_halo, 1, 0)
        own_count += jnp.where(to_own, 1, 0)
    table_ref[HALO_CHUNKS] = (halo_count + CHUNK - 1) >> 3
    table_ref[OWN_CHUNKS] = (own_count + CHUNK - 1) >> 3


def halo_step(rows, split, table_ref, tiles_ref, to_odd, to_even, left_ref, window):
    spread_blocks(jnp.concatenate(two_parts(rows), axis=0) if split else rows, left_ref)
    push_rows(table_ref, False, tiles_ref, left_ref, window, split)
    landed(window, 0, to_odd)
    landed(window, 2, to_even)


def second_kernel(table_ref, tiles_ref, inverse_ref, odd, own, even, to_odd, to_even, left_ref, value_ref, window):
    raw = 0.85 * (own[...] + odd[...] + even[...]) + 0.15
    value_ref[...] = raw
    inverse = inverse_ref[...]
    rows = jnp.concatenate([raw * inverse, inverse], axis=0)
    halo_step(rows, True, table_ref, tiles_ref, to_odd, to_even, left_ref, window)


def chain_kernel(channels, table_ref, tiles_ref, inverse_ref, odd, own, even, to_odd, to_even, left_ref, value_ref, window):
    value = own[...] + odd[...] + even[...]
    value_ref[...] = value
    inverse = inverse_ref[...]
    rows = [value[8 * c : 8 * c + 8] * inverse for c in range(channels)]
    rows = jnp.concatenate(rows, axis=0) if channels > 1 else rows[0]
    halo_step(rows, True, table_ref, tiles_ref, to_odd, to_even, left_ref, window)


def own_kernel(split, table_ref, tiles_ref, left_ref, kept, window):
    push_rows(table_ref, True, tiles_ref, left_ref, window, split)
    landed(window, 1, kept)


def sums_kernel(raw_ref, second_ref, third_ref, odd, own, even, out_ref):
    raw = raw_ref[...]
    second = second_ref[0:8]
    ones_1 = second_ref[8:16]
    third = third_ref[0:8]
    ones_2 = third_ref[8:16]
    fourth = own[...] + odd[...] + even[...]
    wanted = (
        raw * raw,
        second * second, second,
        third * third, third * ones_1, third, ones_1 * ones_1, ones_1,
        fourth * fourth, fourth * ones_2, fourth * ones_1, fourth,
        ones_2 * ones_2, ones_2 * ones_1, ones_2, jnp.zeros_like(raw),
    )
    lines = [jnp.sum(term[:, :128] + term[:, 128:], axis=0, keepdims=True) for term in wanted]
    lines = jnp.sum(jnp.concatenate(lines, axis=0), axis=1, keepdims=True)
    row = lax.broadcasted_iota(jnp.int32, (16, 128), 0)
    lane = lax.broadcasted_iota(jnp.int32, (16, 128), 1)
    out_ref[...] = jnp.sum(jnp.where(row == lane, lines, 0.0), axis=0, keepdims=True)


def scales_of(sums, zones):
    line = jnp.broadcast_to(jnp.sum(sums, axis=0, keepdims=True), (16, 128))
    row = lax.broadcasted_iota(jnp.int32, line.shape, 0)
    lane = lax.broadcasted_iota(jnp.int32, line.shape, 1)
    totals = jnp.sum(jnp.where(row == lane, line, 0.0), axis=1, keepdims=True)
    (r11, c22, c2o, c33, c3p, c3o, pp, po, c44, c4q, c4p, c4o, qq, qp, qo) = (totals[i : i + 1] for i in range(15))
    root = math.sqrt(zones)
    floor = 0.15 * 0.15 * zones
    scale_1 = root / jnp.sqrt(r11)
    a2 = 0.85 * scale_1
    scale_2 = root / jnp.sqrt(a2 * a2 * c22 + 0.3 * a2 * c2o + floor)
    a3 = 0.85 * scale_2 * a2
    p3 = 0.85 * scale_2 * 0.15
    scale_3 = root / jnp.sqrt(
        a3 * a3 * c33 + 2.0 * a3 * (p3 * c3p + 0.15 * c3o) + p3 * p3 * pp + 0.3 * p3 * po + floor
    )
    a4 = 0.85 * scale_3 * a3
    q4 = 0.85 * scale_3 * p3
    p4 = 0.85 * scale_3 * 0.15
    scale_4 = root / jnp.sqrt(
        a4 * a4 * c44 + 2.0 * a4 * (q4 * c4q + p4 * c4p + 0.15 * c4o)
        + q4 * q4 * qq + p4 * p4 * pp + 2.0 * q4 * (p4 * qp + 0.15 * qo) + 0.3 * p4 * po + floor
    )
    return scale_1, scale_2, scale_3, scale_4


def replay_kernel(zones, table_ref, tiles_ref, inverse_ref, sums_ref, raw_ref, second_ref, third_ref, to_odd, to_even, left_ref,
                  scales_ref, window):
    scales = scales_of(sums_ref[...], zones)
    for place, scale in enumerate(scales):
        scales_ref[place : place + 1, :] = jnp.broadcast_to(scale, (1, 128))
    inverse = inverse_ref[...]
    blocks = inverse.shape[0]
    a2 = 0.85 * scales[0]
    a3 = 0.85 * scales[1]

    def own_products(rows):
        spread_blocks(rows, left_ref)
        push_rows(table_ref, True, tiles_ref, left_ref, window, False)
        return jnp.sum(window[blocks : 2 * blocks], axis=1)

    def rounded(rows):
        return rows.astype(BF16).astype(F32)

    plain_2 = (raw_ref[...] * scales[0]) * inverse
    chain_2 = a2 * second_ref[0:blocks] + 0.15
    raw_2 = chain_2 + 0.85 * own_products(rounded(plain_2) - plain_2)
    chain_3 = a3 * (a2 * third_ref[0:blocks] + 0.15 * second_ref[blocks : 2 * blocks]) + 0.15
    weights_3 = rounded((raw_2 * scales[1]) * inverse)
    raw_3 = chain_3 + 0.85 * own_products(weights_3 - (chain_2 * scales[1]) * inverse)
    halo_step((raw_3 * scales[2]) * inverse, False, table_ref, tiles_ref, to_odd, to_even, left_ref, window)


def transposed_kernel(table_ref, tiles_ref, inverse_ref, scales_ref, odd, own, even, probe_ref, to_odd, to_even, pushed_ref, scaled_ref, root_ref, window):
    blocks, chans, width = pushed_ref.shape
    raw = 0.85 * (own[...] + odd[...] + even[...]) + 0.15
    root = jnp.sqrt(raw * scales_ref[3:4, 0:1])
    root_ref[...] = root
    inverse_root = 1.0 / root
    gain = root * inverse_ref[...]
    for block in range(blocks):
        probe = probe_ref[:, block * width : (block + 1) * width].astype(F32)
        pushed_ref[block] = (probe * gain[block : block + 1]).astype(BF16)
        scaled = (probe * inverse_root[block : block + 1]).astype(BF16)
        scaled_ref[block] = scaled
        to_odd[2 * blocks + block] = scaled
        to_even[2 * blocks + block] = scaled
    window[...] = jnp.zeros_like(window)

    def visit(tile, target):
        window[target] += jnp.dot(pushed_ref[tile >> 3], tiles_ref[tile], preferred_element_type=F32)

    for_tiles(table_ref, False, visit)
    for part, out in ((0, to_odd), (2, to_even)):
        for block in range(blocks):
            high, low = two_parts(window[part * blocks + block])
            out[block] = high.astype(BF16)
            out[blocks + block] = low.astype(BF16)


def own_products_kernel(table_ref, tiles_ref, pushed_ref, scaled_ref, kept, forward_ref, window, forward):
    blocks = pushed_ref.shape[0]
    window[...] = jnp.zeros_like(window)
    forward[...] = jnp.zeros_like(forward)

    def visit(tile, target):
        block = tile >> 3
        dead = target == DEAD
        place = jnp.where(dead, blocks, target - blocks)
        matrix = tiles_ref[tile]
        window[place] += jnp.dot(pushed_ref[block], matrix, preferred_element_type=F32)
        left = scaled_ref[jnp.where(dead, 0, place)]
        forward[jnp.where(dead, blocks, block)] += lax.dot_general(left, matrix, LAST_DIMS, preferred_element_type=F32)

    for_tiles(table_ref, True, visit)
    kept[...] = window[0:blocks]
    forward_ref[...] = forward[0:blocks]


def embed_kernel(table_ref, tiles_ref, inverse_ref, root_ref, kept, forward_ref, odd, even, out_ref, gram_ref, forward):
    blocks, chans, width = forward_ref.shape
    forward[0:blocks] = forward_ref[...]
    forward[blocks] = jnp.zeros((chans, width), F32)

    def visit(tile, target):
        dead = target == DEAD
        from_odd = odd[jnp.where(target < blocks, 2 * blocks + target, 2 * blocks)]
        from_even = even[jnp.where((target >= 2 * blocks) & (target < 3 * blocks), target, 2 * blocks)]
        left = jnp.where(target < blocks, from_odd, from_even)
        place = jnp.where(dead, blocks, tile >> 3)
        forward[place] += lax.dot_general(left, tiles_ref[tile], LAST_DIMS, preferred_element_type=F32)

    for_tiles(table_ref, False, visit)
    root = root_ref[...]
    inverse_root = 1.0 / root
    gain = root * inverse_ref[...]
    gram = jnp.zeros((chans, chans), F32)
    for block in range(blocks):
        landing = kept[block]
        for message in (odd, even):
            landing = landing + (message[block].astype(F32) + message[blocks + block].astype(F32))
        embedded = 0.5 * (forward[block] * gain[block : block + 1] + landing * inverse_root[block : block + 1])
        out_ref[:, block * width : (block + 1) * width] = embedded
        gram += lax.dot_general(embedded, embedded, LAST_DIMS, precision=HIGHEST, preferred_element_type=F32)
    gram_ref[...] = jnp.concatenate([gram[8 * i : 8 * i + 8] for i in range(4)], axis=1)


def basis_kernel(gram_ref, embedded_ref, out_ref):
    size = embedded_ref.shape[0]
    row = lax.broadcasted_iota(jnp.int32, (size, size), 0)
    col = lax.broadcasted_iota(jnp.int32, (size, size), 1)
    identity = jnp.where(row == col, 1.0, 0.0)
    gram = jnp.sum(gram_ref[...], axis=0)
    gram = jnp.concatenate([gram[:, size * i : size * (i + 1)] for i in range(4)], axis=0)
    work = jnp.concatenate([gram, identity, jnp.zeros((size, 128 - 2 * size), F32)], axis=1)
    line = lax.broadcasted_iota(jnp.int32, work.shape, 0)
    for first in range(0, size, 4):
        columns = [jnp.broadcast_to(work[:, first + i : first + i + 1], work.shape) for i in range(4)]
        for i in range(4):
            step = first + i
            factor = jnp.where(line > step, columns[i] * (1.0 / columns[i][step : step + 1, :]), 0.0)
            work = work - factor * work[step : step + 1, :]
            for j in range(i + 1, 4):
                columns[j] = columns[j] - factor * columns[j][step : step + 1, :]
    pivots = jnp.sum(work[:, :size] * identity, axis=1, keepdims=True)
    inverse = work[:, size : 2 * size] * (1.0 / jnp.sqrt(pivots))
    out_ref[...] = jnp.dot(inverse, embedded_ref[...], precision=HIGHEST, preferred_element_type=F32)


def call(kernel, name, outs, operands, specs, scratch, out_specs=None, limit=24, flops=0, moved=0):
    return pl.pallas_call(
        kernel,
        out_shape=outs,
        in_specs=specs,
        out_specs=out_specs or [VMEM] * len(outs),
        scratch_shapes=scratch,
        compiler_params=pltpu.CompilerParams(vmem_limit_bytes=limit << 20),
        cost_estimate=pl.CostEstimate(flops=flops, bytes_accessed=moved, transcendentals=0),
        name=name,
    )(*operands)


def per_device(tile_blocks, tile_cols, tile_count, start_mass, probe_block):
    blocks, slots, width = tile_blocks.shape[:3]
    chans = probe_block.shape[0]
    zones = blocks * lax.axis_size(RING) * width

    def rows(channels=1):
        return jax.ShapeDtypeStruct((channels * blocks, width), F32)

    def window(channels, kind=F32, places=3 * blocks + 1):
        return pltpu.VMEM((places, channels, width), kind)

    tiles, target, inverse, to_odd, own, to_even = call(
        load_kernel, "load",
        [pltpu.VMEM((blocks * slots, width, width), BF16), pltpu.SMEM((blocks * slots,), jnp.int32), rows(), rows(), rows(), rows()],
        [pltpu.with_memory_space_constraint(x, pltpu.HBM) for x in (tile_cols, tile_count, tile_blocks, start_mass)],
        [pl.BlockSpec(memory_space=pltpu.HBM)] * 4,
        [
            window(blocks), pltpu.VMEM((blocks, width), F32), pltpu.SMEM(tile_cols.shape, jnp.int32),
            pltpu.SMEM(tile_count.shape, jnp.int32), pltpu.SemaphoreType.DMA((blocks,)), pltpu.SemaphoreType.DMA((2 + blocks,)),
        ],
        [VMEM, SMEM, VMEM, VMEM, VMEM, VMEM],
    )
    tiles = pltpu.with_memory_space_constraint(tiles, pltpu.VMEM)
    odd, even = ring_pairs(to_odd, to_even)
    (table,) = call(
        table_kernel, "table", [pltpu.SMEM((136,), jnp.int32)], [pltpu.with_memory_space_constraint(target, pltpu.SMEM)], [SMEM], [],
        [SMEM], flops=1 << 25, moved=1 << 22,
    )
    table = pltpu.with_memory_space_constraint(table, pltpu.SMEM)

    def step(kernel, name, channels, split, operands, extra):
        height = max(16, channels * blocks * (2 if split else 1))
        left = jax.ShapeDtypeStruct((blocks, height, width), BF16)
        to_odd, to_even, left, *extra = call(
            kernel, name, [rows(channels)] * 2 + [left] + extra, (table, tiles, inverse, *operands),
            [SMEM] + [VMEM] * (2 + len(operands)), [window(channels * blocks)], flops=1 << 24, moved=1 << 21,
        )
        odd, even = ring_pairs(to_odd, to_even)
        (own,) = call(
            functools.partial(own_kernel, split), name + "_own", [rows(channels)], (table, tiles, left), [SMEM] + [VMEM] * 2,
            [window(channels * blocks)], flops=1 << 25, moved=1 << 22,
        )
        return odd, own, even, *extra

    odd, own, even, raw = step(second_kernel, "second", 2, True, (odd, own, even), [rows()])
    odd, own, even, second = step(functools.partial(chain_kernel, 2), "third", 2, True, (odd, own, even), [rows(2)])
    odd, own, even, third = step(functools.partial(chain_kernel, 1), "fourth", 1, True, (odd, own, even), [rows(2)])
    (sums,) = call(
        sums_kernel, "sums", [jax.ShapeDtypeStruct((1, 128), F32)], (raw, second, third, odd, own, even), [VMEM] * 6, []
    )
    sums = chip_parts(sums[0])
    odd, own, even, scales = step(
        functools.partial(replay_kernel, zones), "replay", 1, False, (sums, raw, second, third),
        [jax.ShapeDtypeStruct((8, 128), F32)],
    )

    message = jax.ShapeDtypeStruct((3 * blocks, chans, width), BF16)
    narrow = jax.ShapeDtypeStruct((blocks, chans, width), BF16)
    wide = jax.ShapeDtypeStruct((blocks, chans, width), F32)
    to_odd, to_even, pushed, scaled, root = call(
        transposed_kernel, "transposed", [message, message, narrow, narrow, rows()],
        (table, tiles, inverse, scales, odd, own, even, probe_block), [SMEM] + [VMEM] * 7, [window(chans)],
    )
    odd, even = ring_pairs(to_odd, to_even)
    kept, forward = call(
        own_products_kernel, "own_products", [wide, wide], (table, tiles, pushed, scaled), [SMEM] + [VMEM] * 3,
        [window(chans, places=blocks + 1)] * 2, flops=1 << 28, moved=1 << 23,
    )
    embedded, gram = call(
        embed_kernel, "embed",
        [jax.ShapeDtypeStruct((chans, blocks * width), F32), jax.ShapeDtypeStruct((8, 128), F32)],
        (table, tiles, inverse, root, kept, forward, odd, even), [SMEM] + [VMEM] * 7, [window(chans, places=blocks + 1)],
    )
    (basis,) = call(
        basis_kernel, "basis", [jax.ShapeDtypeStruct((chans, blocks * width), F32)], (plane_parts(gram), embedded), [VMEM] * 2, []
    )
    return basis


def solution(mesh):
    return jax.shard_map(
        per_device,
        mesh=mesh,
        in_specs=(P(RING, None, None, None), P(RING, None), P(RING), P(RING), P(None, RING)),
        out_specs=P(None, RING),
        check_vma=False,
    )
```

```python
import functools
import math

import jax
import jax.numpy as jnp
from jax import lax
from jax.experimental import pallas as pl
from jax.experimental.pallas import tpu as pltpu
from jax.sharding import PartitionSpec as P

RING = ("rows", "cols")
F32 = jnp.float32
BF16 = jnp.bfloat16
HIGHEST = lax.Precision.HIGHEST
LAST_DIMS = (((1,), (1,)), ((), ()))
SMEM = pl.BlockSpec(memory_space=pltpu.SMEM)
VMEM = pl.BlockSpec(memory_space=pltpu.VMEM)
CHUNK = 8
DEAD = 24
HALO_CHUNKS = 128
OWN_CHUNKS = 129
SPARE = 130


def swap(shard, axis, partner):
    count = lax.axis_size(axis)
    return lax.ppermute(shard, axis, [(i, partner(i) % count) for i in range(count)])


def ring_pairs(shard_odd, shard_even):
    got_odd = swap(shard_odd, RING, lambda i: i + 1 if i % 2 else i - 1)
    got_even = swap(shard_even, RING, lambda i: i - 1 if i % 2 else i + 1)
    return got_odd, got_even


def gathered(part, axis, groups):
    spread = jnp.broadcast_to(part[None], (len(groups[0]), *part.shape))
    return lax.all_to_all(spread, axis, 0, 0, tiled=True, axis_index_groups=groups)


def chip_parts(part):
    part = part + swap(part, "rows", lambda i: i ^ 1)
    cols = lax.axis_size("cols")
    devices = lax.axis_size(RING)
    groups = [[i for i in range(devices) if (i // cols) % 2 == core] for core in (0, 1)]
    return gathered(part, RING, groups)


def plane_parts(part):
    part = part + swap(part, "rows", lambda i: i ^ 1)
    part = part + sum(swap(part, "cols", lambda i, d=d: i ^ d) for d in (1, 2, 3))
    groups = [list(range(core, lax.axis_size("rows"), 2)) for core in (0, 1)]
    return gathered(part, "rows", groups)


def two_parts(value):
    high = value.astype(BF16).astype(F32)
    return high, value - high


def spread_blocks(rows, left_ref):
    blocks, height = left_ref.shape[:2]
    if rows.shape[0] < height:
        rows = jnp.concatenate([rows, jnp.zeros((height - rows.shape[0], rows.shape[1]), F32)], axis=0)
    owner = lax.broadcasted_iota(jnp.int32, rows.shape, 0) % blocks
    for block in range(blocks):
        left_ref[block] = jnp.where(owner == block, rows, 0.0).astype(BF16)


def for_tiles(table_ref, own, visit):
    first = 64 if own else 0

    def chunk(number, carry):
        for place in range(CHUNK):
            entry = table_ref[first + number * CHUNK + place]
            visit(entry >> 5, entry & 31)
        return carry

    lax.fori_loop(0, table_ref[OWN_CHUNKS if own else HALO_CHUNKS], chunk, 0)


def push_rows(table_ref, own, tiles_ref, left_ref, window, split):
    height = window.shape[1]
    window[...] = jnp.zeros_like(window)

    def visit(tile, target):
        product = jnp.dot(left_ref[tile >> 3], tiles_ref[tile], preferred_element_type=F32)
        if split:
            product = product[:height] + product[height : 2 * height]
        window[target] += product[:height]

    for_tiles(table_ref, own, visit)


def landed(window, part, out):
    for channel in range(out.shape[0] // 8):
        rows = slice(channel * 8, (channel + 1) * 8)
        out[rows, :] = jnp.sum(window[part * 8 : (part + 1) * 8, rows, :], axis=1)


def load_kernel(cols_hbm, count_hbm, tiles_hbm, start_hbm, tiles_ref, table_ref, inverse_ref, to_odd, to_even, left_ref,
                window, start_ref, cols_ref, count_ref, sems, small_sems):
    blocks, slots, width = tiles_hbm.shape[:3]
    small = [
        pltpu.make_async_copy(cols_hbm, cols_ref, small_sems.at[0]),
        pltpu.make_async_copy(count_hbm, count_ref, small_sems.at[1]),
    ]
    small += [
        pltpu.make_async_copy(start_hbm.at[pl.ds(b * width, width)], start_ref.at[b], small_sems.at[2 + b]) for b in range(blocks)
    ]
    copies = [
        pltpu.make_async_copy(tiles_hbm.at[b], tiles_ref.at[pl.ds(b * slots, slots)], sems.at[b]) for b in range(blocks)
    ]
    for copy in small + copies:
        copy.start()
    total_blocks = blocks * lax.axis_size("rows") * lax.axis_size("cols")
    place = lax.axis_index("rows") * lax.axis_size("cols") + lax.axis_index("cols")
    swapped = place % 2 == 1
    for entry in range(128):
        table_ref[entry] = DEAD
    for copy in small:
        copy.wait()
    halo_count, own_count = jnp.int32(0), jnp.int32(0)
    for block in range(blocks):
        for slot in range(slots):
            target = cols_ref[block, slot] - place * blocks + blocks
            target = jnp.where(target < 0, target + total_blocks, target)
            target = jnp.where(target >= total_blocks, target - total_blocks, target)
            own = (target >= blocks) & (target < 2 * blocks)
            flipped = jnp.where(target < blocks, target + 2 * blocks, target - 2 * blocks)
            target = jnp.where(swapped & jnp.logical_not(own), flipped, target)
            live = slot < count_ref[block]
            to_own = live & own
            to_halo = live & jnp.logical_not(own)
            entry = target + (block * slots + slot) * 32
            table_ref[jnp.where(to_halo, halo_count, jnp.where(to_own, 64 + own_count, SPARE))] = entry
            halo_count += jnp.where(to_halo, 1, 0)
            own_count += jnp.where(to_own, 1, 0)
    table_ref[HALO_CHUNKS] = (halo_count + CHUNK - 1) >> 3
    table_ref[OWN_CHUNKS] = (own_count + CHUNK - 1) >> 3

    ones = jnp.ones((16, 128), BF16)

    def folded_tiles(block):
        folded = jnp.zeros((width, 128), F32)
        for slot in range(slots):
            tile = tiles_ref[block * slots + slot].astype(F32)
            folded = folded + (tile[:, :128] + tile[:, 128:]) * jnp.where(slot < count_ref[block], 1.0, 0.0)
        return folded

    def row_sums(folded):
        total = jnp.zeros((16, width), F32)
        for _ in range(3):
            part = folded.astype(BF16)
            folded = folded - part.astype(F32)
            total = total + lax.dot_general(ones, part, LAST_DIMS, preferred_element_type=F32)
        return total[0:1]

    sums = []
    before = None
    for block in range(blocks):
        copies[block].wait()
        folded = folded_tiles(block)
        if before is not None:
            sums.append(row_sums(before))
        before = folded
    sums.append(row_sums(before))
    inverse = 1.0 / jnp.concatenate(sums, axis=0)
    inverse_ref[...] = inverse
    halo_step(start_ref[...] * inverse, False, table_ref, tiles_ref, to_odd, to_even, left_ref, window)


def halo_step(rows, split, table_ref, tiles_ref, to_odd, to_even, left_ref, window):
    spread_blocks(jnp.concatenate(two_parts(rows), axis=0) if split else rows, left_ref)
    push_rows(table_ref, False, tiles_ref, left_ref, window, split)
    landed(window, 0, to_odd)
    landed(window, 2, to_even)


def second_kernel(table_ref, tiles_ref, inverse_ref, odd, own, even, to_odd, to_even, left_ref, value_ref, window):
    raw = 0.85 * (own[...] + odd[...] + even[...]) + 0.15
    value_ref[...] = raw
    inverse = inverse_ref[...]
    rows = jnp.concatenate([raw * inverse, inverse], axis=0)
    halo_step(rows, True, table_ref, tiles_ref, to_odd, to_even, left_ref, window)


def chain_kernel(channels, table_ref, tiles_ref, inverse_ref, odd, own, even, to_odd, to_even, left_ref, value_ref, window):
    value = own[...] + odd[...] + even[...]
    value_ref[...] = value
    inverse = inverse_ref[...]
    rows = [value[8 * c : 8 * c + 8] * inverse for c in range(channels)]
    rows = jnp.concatenate(rows, axis=0) if channels > 1 else rows[0]
    halo_step(rows, True, table_ref, tiles_ref, to_odd, to_even, left_ref, window)


def own_kernel(split, table_ref, tiles_ref, left_ref, kept, window):
    push_rows(table_ref, True, tiles_ref, left_ref, window, split)
    landed(window, 1, kept)


def sums_kernel(raw_ref, second_ref, third_ref, odd, own, even, out_ref):
    raw = raw_ref[...]
    second = second_ref[0:8]
    ones_1 = second_ref[8:16]
    third = third_ref[0:8]
    ones_2 = third_ref[8:16]
    fourth = own[...] + odd[...] + even[...]
    wanted = (
        raw * raw,
        second * second, second,
        third * third, third * ones_1, third, ones_1 * ones_1, ones_1,
        fourth * fourth, fourth * ones_2, fourth * ones_1, fourth,
        ones_2 * ones_2, ones_2 * ones_1, ones_2, jnp.zeros_like(raw),
    )
    lines = [jnp.sum(term[:, :128] + term[:, 128:], axis=0, keepdims=True) for term in wanted]
    lines = jnp.sum(jnp.concatenate(lines, axis=0), axis=1, keepdims=True)
    row = lax.broadcasted_iota(jnp.int32, (16, 128), 0)
    lane = lax.broadcasted_iota(jnp.int32, (16, 128), 1)
    out_ref[...] = jnp.sum(jnp.where(row == lane, lines, 0.0), axis=0, keepdims=True)


def scales_of(sums, zones):
    line = jnp.broadcast_to(jnp.sum(sums, axis=0, keepdims=True), (16, 128))
    row = lax.broadcasted_iota(jnp.int32, line.shape, 0)
    lane = lax.broadcasted_iota(jnp.int32, line.shape, 1)
    totals = jnp.sum(jnp.where(row == lane, line, 0.0), axis=1, keepdims=True)
    (r11, c22, c2o, c33, c3p, c3o, pp, po, c44, c4q, c4p, c4o, qq, qp, qo) = (totals[i : i + 1] for i in range(15))
    root = math.sqrt(zones)
    floor = 0.15 * 0.15 * zones
    scale_1 = root / jnp.sqrt(r11)
    a2 = 0.85 * scale_1
    scale_2 = root / jnp.sqrt(a2 * a2 * c22 + 0.3 * a2 * c2o + floor)
    a3 = 0.85 * scale_2 * a2
    p3 = 0.85 * scale_2 * 0.15
    scale_3 = root / jnp.sqrt(
        a3 * a3 * c33 + 2.0 * a3 * (p3 * c3p + 0.15 * c3o) + p3 * p3 * pp + 0.3 * p3 * po + floor
    )
    a4 = 0.85 * scale_3 * a3
    q4 = 0.85 * scale_3 * p3
    p4 = 0.85 * scale_3 * 0.15
    scale_4 = root / jnp.sqrt(
        a4 * a4 * c44 + 2.0 * a4 * (q4 * c4q + p4 * c4p + 0.15 * c4o)
        + q4 * q4 * qq + p4 * p4 * pp + 2.0 * q4 * (p4 * qp + 0.15 * qo) + 0.3 * p4 * po + floor
    )
    return scale_1, scale_2, scale_3, scale_4


def replay_kernel(zones, table_ref, tiles_ref, inverse_ref, sums_ref, raw_ref, second_ref, third_ref, to_odd, to_even, left_ref,
                  scales_ref, window):
    scales = scales_of(sums_ref[...], zones)
    for place, scale in enumerate(scales):
        scales_ref[place : place + 1, :] = jnp.broadcast_to(scale, (1, 128))
    inverse = inverse_ref[...]
    blocks = inverse.shape[0]
    a2 = 0.85 * scales[0]
    a3 = 0.85 * scales[1]

    def own_products(rows):
        spread_blocks(rows, left_ref)
        push_rows(table_ref, True, tiles_ref, left_ref, window, False)
        return jnp.sum(window[blocks : 2 * blocks], axis=1)

    def rounded(rows):
        return rows.astype(BF16).astype(F32)

    plain_2 = (raw_ref[...] * scales[0]) * inverse
    chain_2 = a2 * second_ref[0:blocks] + 0.15
    raw_2 = chain_2 + 0.85 * own_products(rounded(plain_2) - plain_2)
    chain_3 = a3 * (a2 * third_ref[0:blocks] + 0.15 * second_ref[blocks : 2 * blocks]) + 0.15
    weights_3 = rounded((raw_2 * scales[1]) * inverse)
    raw_3 = chain_3 + 0.85 * own_products(weights_3 - (chain_2 * scales[1]) * inverse)
    halo_step((raw_3 * scales[2]) * inverse, False, table_ref, tiles_ref, to_odd, to_even, left_ref, window)


def transposed_kernel(table_ref, tiles_ref, inverse_ref, scales_ref, odd, own, even, probe_ref, to_odd, to_even, pushed_ref, scaled_ref, root_ref, window):
    blocks, chans, width = pushed_ref.shape
    raw = 0.85 * (own[...] + odd[...] + even[...]) + 0.15
    root = jnp.sqrt(raw * scales_ref[3:4, 0:1])
    root_ref[...] = root
    inverse_root = 1.0 / root
    gain = root * inverse_ref[...]
    for block in range(blocks):
        probe = probe_ref[:, block * width : (block + 1) * width].astype(F32)
        pushed_ref[block] = (probe * gain[block : block + 1]).astype(BF16)
        scaled = (probe * inverse_root[block : block + 1]).astype(BF16)
        scaled_ref[block] = scaled
        to_odd[2 * blocks + block] = scaled
        to_even[2 * blocks + block] = scaled
    window[...] = jnp.zeros_like(window)

    def visit(tile, target):
        window[target] += jnp.dot(pushed_ref[tile >> 3], tiles_ref[tile], preferred_element_type=F32)

    for_tiles(table_ref, False, visit)
    for part, out in ((0, to_odd), (2, to_even)):
        for block in range(blocks):
            high, low = two_parts(window[part * blocks + block])
            out[block] = high.astype(BF16)
            out[blocks + block] = low.astype(BF16)


def own_products_kernel(table_ref, tiles_ref, pushed_ref, scaled_ref, kept, forward_ref, window, forward):
    blocks = pushed_ref.shape[0]
    window[...] = jnp.zeros_like(window)
    forward[...] = jnp.zeros_like(forward)

    def visit(tile, target):
        block = tile >> 3
        dead = target == DEAD
        place = jnp.where(dead, blocks, target - blocks)
        matrix = tiles_ref[tile]
        window[place] += jnp.dot(pushed_ref[block], matrix, preferred_element_type=F32)
        left = scaled_ref[jnp.where(dead, 0, place)]
        forward[jnp.where(dead, blocks, block)] += lax.dot_general(left, matrix, LAST_DIMS, preferred_element_type=F32)

    for_tiles(table_ref, True, visit)
    kept[...] = window[0:blocks]
    forward_ref[...] = forward[0:blocks]


def embed_kernel(table_ref, tiles_ref, inverse_ref, root_ref, kept, forward_ref, odd, even, out_ref, gram_ref, forward):
    blocks, chans, width = forward_ref.shape
    forward[0:blocks] = forward_ref[...]
    forward[blocks] = jnp.zeros((chans, width), F32)

    def visit(tile, target):
        dead = target == DEAD
        from_odd = odd[jnp.where(target < blocks, 2 * blocks + target, 2 * blocks)]
        from_even = even[jnp.where((target >= 2 * blocks) & (target < 3 * blocks), target, 2 * blocks)]
        left = jnp.where(target < blocks, from_odd, from_even)
        place = jnp.where(dead, blocks, tile >> 3)
        forward[place] += lax.dot_general(left, tiles_ref[tile], LAST_DIMS, preferred_element_type=F32)

    for_tiles(table_ref, False, visit)
    root = root_ref[...]
    inverse_root = 1.0 / root
    gain = root * inverse_ref[...]
    gram = jnp.zeros((chans, chans), F32)
    for block in range(blocks):
        landing = kept[block]
        for message in (odd, even):
            landing = landing + (message[block].astype(F32) + message[blocks + block].astype(F32))
        embedded = 0.5 * (forward[block] * gain[block : block + 1] + landing * inverse_root[block : block + 1])
        out_ref[:, block * width : (block + 1) * width] = embedded
        gram += lax.dot_general(embedded, embedded, LAST_DIMS, precision=HIGHEST, preferred_element_type=F32)
    gram_ref[...] = jnp.concatenate([gram[8 * i : 8 * i + 8] for i in range(4)], axis=1)


def basis_kernel(gram_ref, embedded_ref, out_hbm, out_ref, sems):
    size = embedded_ref.shape[0]
    row = lax.broadcasted_iota(jnp.int32, (size, size), 0)
    col = lax.broadcasted_iota(jnp.int32, (size, size), 1)
    identity = jnp.where(row == col, 1.0, 0.0)
    gram = jnp.sum(gram_ref[...], axis=0)
    gram = jnp.concatenate([gram[:, size * i : size * (i + 1)] for i in range(4)], axis=0)
    work = jnp.concatenate([gram, identity, jnp.zeros((size, 128 - 2 * size), F32)], axis=1)
    line = lax.broadcasted_iota(jnp.int32, work.shape, 0)
    for first in range(0, size, 16):
        columns = [jnp.broadcast_to(work[:, first + i : first + i + 1], work.shape) for i in range(16)]
        for i in range(16):
            step = first + i
            factor = jnp.where(line > step, columns[i] * (1.0 / columns[i][step : step + 1, :]), 0.0)
            work = work - factor * work[step : step + 1, :]
            for j in range(i + 1, 16):
                columns[j] = columns[j] - factor * columns[j][step : step + 1, :]
    pivots = jnp.sum(work[:, :size] * identity, axis=1, keepdims=True)
    inverse = work[:, size : 2 * size] * (1.0 / jnp.sqrt(pivots))
    parts = sems.shape[0]
    width = embedded_ref.shape[1] // parts
    copies = []
    for part in range(parts):
        span = pl.ds(part * width, width)
        out_ref[:, span] = jnp.dot(inverse, embedded_ref[:, span], precision=HIGHEST, preferred_element_type=F32)
        copies.append(pltpu.make_async_copy(out_ref.at[:, span], out_hbm.at[:, span], sems.at[part]))
        copies[-1].start()
    for copy in copies:
        copy.wait()


def call(kernel, name, outs, operands, specs, scratch, out_specs=None, limit=24, flops=0, moved=0):
    return pl.pallas_call(
        kernel,
        out_shape=outs,
        in_specs=specs,
        out_specs=out_specs or [VMEM] * len(outs),
        scratch_shapes=scratch,
        compiler_params=pltpu.CompilerParams(vmem_limit_bytes=limit << 20),
        cost_estimate=pl.CostEstimate(flops=flops, bytes_accessed=moved, transcendentals=0),
        name=name,
    )(*operands)


def per_device(tile_blocks, tile_cols, tile_count, start_mass, probe_block):
    blocks, slots, width = tile_blocks.shape[:3]
    chans = probe_block.shape[0]
    zones = blocks * lax.axis_size(RING) * width

    def rows(channels=1):
        return jax.ShapeDtypeStruct((channels * blocks, width), F32)

    def window(channels, kind=F32, places=3 * blocks + 1):
        return pltpu.VMEM((places, channels, width), kind)

    tiles, table, inverse, to_odd, to_even, left = call(
        load_kernel, "load",
        [
            pltpu.VMEM((blocks * slots, width, width), BF16), pltpu.SMEM((136,), jnp.int32), rows(), rows(), rows(),
            jax.ShapeDtypeStruct((blocks, 16, width), BF16),
        ],
        [pltpu.with_memory_space_constraint(x, pltpu.HBM) for x in (tile_cols, tile_count, tile_blocks, start_mass)],
        [pl.BlockSpec(memory_space=pltpu.HBM)] * 4,
        [
            window(blocks), pltpu.VMEM((blocks, width), F32), pltpu.SMEM(tile_cols.shape, jnp.int32),
            pltpu.SMEM(tile_count.shape, jnp.int32), pltpu.SemaphoreType.DMA((blocks,)), pltpu.SemaphoreType.DMA((2 + blocks,)),
        ],
        [VMEM, SMEM, VMEM, VMEM, VMEM, VMEM],
    )
    tiles = pltpu.with_memory_space_constraint(tiles, pltpu.VMEM)
    table = pltpu.with_memory_space_constraint(table, pltpu.SMEM)

    def exchange(to_odd, to_even, left, name, channels, split):
        odd, even = ring_pairs(to_odd, to_even)
        (own,) = call(
            functools.partial(own_kernel, split), name + "_own", [rows(channels)], (table, tiles, left), [SMEM] + [VMEM] * 2,
            [window(channels * blocks)], flops=1 << 25, moved=1 << 22,
        )
        return odd, own, even

    odd, own, even = exchange(to_odd, to_even, left, "first", 1, False)

    def step(kernel, name, channels, split, operands, extra):
        height = max(16, channels * blocks * (2 if split else 1))
        left = jax.ShapeDtypeStruct((blocks, height, width), BF16)
        to_odd, to_even, left, *extra = call(
            kernel, name, [rows(channels)] * 2 + [left] + extra, (table, tiles, inverse, *operands),
            [SMEM] + [VMEM] * (2 + len(operands)), [window(channels * blocks)], flops=1 << 24, moved=1 << 21,
        )
        return *exchange(to_odd, to_even, left, name, channels, split), *extra

    odd, own, even, raw = step(second_kernel, "second", 2, True, (odd, own, even), [rows()])
    odd, own, even, second = step(functools.partial(chain_kernel, 2), "third", 2, True, (odd, own, even), [rows(2)])
    odd, own, even, third = step(functools.partial(chain_kernel, 1), "fourth", 1, True, (odd, own, even), [rows(2)])
    (sums,) = call(
        sums_kernel, "sums", [jax.ShapeDtypeStruct((1, 128), F32)], (raw, second, third, odd, own, even), [VMEM] * 6, []
    )
    sums = chip_parts(sums[0])
    odd, own, even, scales = step(
        functools.partial(replay_kernel, zones), "replay", 1, False, (sums, raw, second, third),
        [jax.ShapeDtypeStruct((8, 128), F32)],
    )

    message = jax.ShapeDtypeStruct((3 * blocks, chans, width), BF16)
    narrow = jax.ShapeDtypeStruct((blocks, chans, width), BF16)
    wide = jax.ShapeDtypeStruct((blocks, chans, width), F32)
    to_odd, to_even, pushed, scaled, root = call(
        transposed_kernel, "transposed", [message, message, narrow, narrow, rows()],
        (table, tiles, inverse, scales, odd, own, even, probe_block), [SMEM] + [VMEM] * 7, [window(chans)],
    )
    odd, even = ring_pairs(to_odd, to_even)
    kept, forward = call(
        own_products_kernel, "own_products", [wide, wide], (table, tiles, pushed, scaled), [SMEM] + [VMEM] * 3,
        [window(chans, places=blocks + 1)] * 2, flops=1 << 28, moved=1 << 23,
    )
    embedded, gram = call(
        embed_kernel, "embed",
        [jax.ShapeDtypeStruct((chans, blocks * width), F32), jax.ShapeDtypeStruct((8, 128), F32)],
        (table, tiles, inverse, root, kept, forward, odd, even), [SMEM] + [VMEM] * 7, [window(chans, places=blocks + 1)],
    )
    (basis,) = call(
        basis_kernel, "basis", [pltpu.HBM((chans, blocks * width), F32)], (plane_parts(gram), embedded), [VMEM] * 2,
        [pltpu.VMEM((chans, blocks * width), F32), pltpu.SemaphoreType.DMA((4,))], [pl.BlockSpec(memory_space=pltpu.HBM)],
    )
    return basis


def solution(mesh):
    return jax.shard_map(
        per_device,
        mesh=mesh,
        in_specs=(P(RING, None, None, None), P(RING, None), P(RING), P(RING), P(None, RING)),
        out_specs=P(None, RING),
        check_vma=False,
    )
```

```python
import functools
import math

import jax
import jax.numpy as jnp
from jax import lax
from jax.experimental import pallas as pl
from jax.experimental.pallas import tpu as pltpu
from jax.sharding import PartitionSpec as P

RING = ("rows", "cols")
F32 = jnp.float32
BF16 = jnp.bfloat16
HIGHEST = lax.Precision.HIGHEST
LAST_DIMS = (((1,), (1,)), ((), ()))
SMEM = pl.BlockSpec(memory_space=pltpu.SMEM)
VMEM = pl.BlockSpec(memory_space=pltpu.VMEM)
CHUNK = 8
DEAD = 24
ODD, EVEN, OWN = 0, 1, 2
ROOM = 64
CHUNKS = 3 * ROOM
SPARE = CHUNKS + 3
TABLE = CHUNKS + 8


def swap(shard, axis, partner):
    count = lax.axis_size(axis)
    return lax.ppermute(shard, axis, [(i, partner(i) % count) for i in range(count)])


def swap_odd(shard):
    return swap(shard, RING, lambda i: i + 1 if i % 2 else i - 1)


def swap_even(shard):
    return swap(shard, RING, lambda i: i - 1 if i % 2 else i + 1)


def gathered(part, axis, groups):
    spread = jnp.broadcast_to(part[None], (len(groups[0]), *part.shape))
    return lax.all_to_all(spread, axis, 0, 0, tiled=True, axis_index_groups=groups)


def chip_parts(part):
    part = part + swap(part, "rows", lambda i: i ^ 1)
    cols = lax.axis_size("cols")
    devices = lax.axis_size(RING)
    groups = [[i for i in range(devices) if (i // cols) % 2 == core] for core in (0, 1)]
    return gathered(part, RING, groups)


def plane_parts(part):
    part = part + swap(part, "rows", lambda i: i ^ 1)
    part = part + sum(swap(part, "cols", lambda i, d=d: i ^ d) for d in (1, 2, 3))
    groups = [list(range(core, lax.axis_size("rows"), 2)) for core in (0, 1)]
    return gathered(part, "rows", groups)


def two_parts(value):
    high = value.astype(BF16).astype(F32)
    return high, value - high


def spread_blocks(rows, left_ref):
    blocks, height = left_ref.shape[:2]
    if rows.shape[0] < height:
        rows = jnp.concatenate([rows, jnp.zeros((height - rows.shape[0], rows.shape[1]), F32)], axis=0)
    owner = lax.broadcasted_iota(jnp.int32, rows.shape, 0) % blocks
    for block in range(blocks):
        left_ref[block] = jnp.where(owner == block, rows, 0.0).astype(BF16)


def for_tiles(table_ref, lists, visit):
    for number in lists:

        def chunk(place, carry, first=number * ROOM):
            for offset in range(CHUNK):
                entry = table_ref[first + place * CHUNK + offset]
                visit(entry >> 5, entry & 31)
            return carry

        lax.fori_loop(0, table_ref[CHUNKS + number], chunk, 0)


def push_rows(table_ref, lists, tiles_ref, left_ref, window, split):
    height = window.shape[1]
    window[...] = jnp.zeros_like(window)

    def visit(tile, target):
        product = jnp.dot(left_ref[tile >> 3], tiles_ref[tile], preferred_element_type=F32)
        if split:
            product = product[:height] + product[height : 2 * height]
        window[target] += product[:height]

    for_tiles(table_ref, lists, visit)


def landed(window, part, out):
    for channel in range(out.shape[0] // 8):
        rows = slice(channel * 8, (channel + 1) * 8)
        out[rows, :] = jnp.sum(window[part * 8 : (part + 1) * 8, rows, :], axis=1)


def load_kernel(cols_hbm, count_hbm, tiles_hbm, start_hbm, tiles_ref, table_ref, inverse_ref, to_odd, left_ref, to_even,
                window, start_ref, cols_ref, count_ref, sems, small_sems):
    blocks, slots, width = tiles_hbm.shape[:3]
    small = [
        pltpu.make_async_copy(cols_hbm, cols_ref, small_sems.at[0]),
        pltpu.make_async_copy(count_hbm, count_ref, small_sems.at[1]),
    ]
    small += [
        pltpu.make_async_copy(start_hbm.at[pl.ds(b * width, width)], start_ref.at[b], small_sems.at[2 + b]) for b in range(blocks)
    ]
    copies = [
        pltpu.make_async_copy(tiles_hbm.at[b], tiles_ref.at[pl.ds(b * slots, slots)], sems.at[b]) for b in range(blocks)
    ]
    for copy in small + copies:
        copy.start()
    total_blocks = blocks * lax.axis_size("rows") * lax.axis_size("cols")
    place = lax.axis_index("rows") * lax.axis_size("cols") + lax.axis_index("cols")
    swapped = place % 2 == 1
    for entry in range(CHUNKS):
        table_ref[entry] = DEAD
    for copy in small:
        copy.wait()
    counts = [jnp.int32(0)] * 3
    for block in range(blocks):
        for slot in range(slots):
            target = cols_ref[block, slot] - place * blocks + blocks
            target = jnp.where(target < 0, target + total_blocks, target)
            target = jnp.where(target >= total_blocks, target - total_blocks, target)
            own = (target >= blocks) & (target < 2 * blocks)
            flipped = jnp.where(target < blocks, target + 2 * blocks, target - 2 * blocks)
            target = jnp.where(swapped & jnp.logical_not(own), flipped, target)
            live = slot < count_ref[block]
            entry = target + (block * slots + slot) * 32
            chosen = [live & (target < blocks), live & (target >= 2 * blocks), live & own]
            place_of = SPARE
            for number in (ODD, EVEN, OWN):
                place_of = jnp.where(chosen[number], number * ROOM + counts[number], place_of)
                counts[number] += jnp.where(chosen[number], 1, 0)
            table_ref[place_of] = entry
    for number in (ODD, EVEN, OWN):
        table_ref[CHUNKS + number] = (counts[number] + CHUNK - 1) >> 3

    ones = jnp.ones((16, 128), BF16)

    def folded_tiles(block):
        folded = jnp.zeros((width, 128), F32)
        for slot in range(slots):
            tile = tiles_ref[block * slots + slot].astype(F32)
            folded = folded + (tile[:, :128] + tile[:, 128:]) * jnp.where(slot < count_ref[block], 1.0, 0.0)
        return folded

    def row_sums(folded):
        total = jnp.zeros((16, width), F32)
        for _ in range(3):
            part = folded.astype(BF16)
            folded = folded - part.astype(F32)
            total = total + lax.dot_general(ones, part, LAST_DIMS, preferred_element_type=F32)
        return total[0:1]

    sums = []
    before = None
    for block in range(blocks):
        copies[block].wait()
        folded = folded_tiles(block)
        if before is not None:
            sums.append(row_sums(before))
        before = folded
    sums.append(row_sums(before))
    inverse = 1.0 / jnp.concatenate(sums, axis=0)
    inverse_ref[...] = inverse
    halo_step(start_ref[...] * inverse, False, table_ref, tiles_ref, to_odd, left_ref, to_even, window)


def halo_step(rows, split, table_ref, tiles_ref, to_odd, left_ref, *rest):
    window = rest[-1]
    spread_blocks(jnp.concatenate(two_parts(rows), axis=0) if split else rows, left_ref)
    push_rows(table_ref, (ODD,) if len(rest) == 1 else (ODD, EVEN), tiles_ref, left_ref, window, split)
    landed(window, 0, to_odd)
    if len(rest) > 1:
        landed(window, 2, rest[0])


def second_kernel(table_ref, tiles_ref, inverse_ref, odd, own, even, to_odd, left_ref, value_ref, *rest):
    raw = 0.85 * (own[...] + odd[...] + even[...]) + 0.15
    value_ref[...] = raw
    inverse = inverse_ref[...]
    rows = jnp.concatenate([raw * inverse, inverse], axis=0)
    halo_step(rows, True, table_ref, tiles_ref, to_odd, left_ref, *rest)


def chain_kernel(channels, table_ref, tiles_ref, inverse_ref, odd, own, even, to_odd, left_ref, value_ref, *rest):
    value = own[...] + odd[...] + even[...]
    value_ref[...] = value
    inverse = inverse_ref[...]
    rows = [value[8 * c : 8 * c + 8] * inverse for c in range(channels)]
    rows = jnp.concatenate(rows, axis=0) if channels > 1 else rows[0]
    halo_step(rows, True, table_ref, tiles_ref, to_odd, left_ref, *rest)


def own_kernel(split, table_ref, tiles_ref, left_ref, kept, *rest):
    window = rest[-1]
    push_rows(table_ref, (OWN,) if len(rest) == 1 else (EVEN, OWN), tiles_ref, left_ref, window, split)
    landed(window, 1, kept)
    if len(rest) > 1:
        landed(window, 2, rest[0])


def sums_kernel(raw_ref, second_ref, third_ref, odd, own, even, out_ref):
    raw = raw_ref[...]
    second = second_ref[0:8]
    ones_1 = second_ref[8:16]
    third = third_ref[0:8]
    ones_2 = third_ref[8:16]
    fourth = own[...] + odd[...] + even[...]
    wanted = (
        raw * raw,
        second * second, second,
        third * third, third * ones_1, third, ones_1 * ones_1, ones_1,
        fourth * fourth, fourth * ones_2, fourth * ones_1, fourth,
        ones_2 * ones_2, ones_2 * ones_1, ones_2, jnp.zeros_like(raw),
    )
    lines = [jnp.sum(term[:, :128] + term[:, 128:], axis=0, keepdims=True) for term in wanted]
    lines = jnp.sum(jnp.concatenate(lines, axis=0), axis=1, keepdims=True)
    row = lax.broadcasted_iota(jnp.int32, (16, 128), 0)
    lane = lax.broadcasted_iota(jnp.int32, (16, 128), 1)
    out_ref[...] = jnp.sum(jnp.where(row == lane, lines, 0.0), axis=0, keepdims=True)


def scales_of(sums, zones):
    line = jnp.broadcast_to(jnp.sum(sums, axis=0, keepdims=True), (16, 128))
    row = lax.broadcasted_iota(jnp.int32, line.shape, 0)
    lane = lax.broadcasted_iota(jnp.int32, line.shape, 1)
    totals = jnp.sum(jnp.where(row == lane, line, 0.0), axis=1, keepdims=True)
    (r11, c22, c2o, c33, c3p, c3o, pp, po, c44, c4q, c4p, c4o, qq, qp, qo) = (totals[i : i + 1] for i in range(15))
    root = math.sqrt(zones)
    floor = 0.15 * 0.15 * zones
    scale_1 = root / jnp.sqrt(r11)
    a2 = 0.85 * scale_1
    scale_2 = root / jnp.sqrt(a2 * a2 * c22 + 0.3 * a2 * c2o + floor)
    a3 = 0.85 * scale_2 * a2
    p3 = 0.85 * scale_2 * 0.15
    scale_3 = root / jnp.sqrt(
        a3 * a3 * c33 + 2.0 * a3 * (p3 * c3p + 0.15 * c3o) + p3 * p3 * pp + 0.3 * p3 * po + floor
    )
    a4 = 0.85 * scale_3 * a3
    q4 = 0.85 * scale_3 * p3
    p4 = 0.85 * scale_3 * 0.15
    scale_4 = root / jnp.sqrt(
        a4 * a4 * c44 + 2.0 * a4 * (q4 * c4q + p4 * c4p + 0.15 * c4o)
        + q4 * q4 * qq + p4 * p4 * pp + 2.0 * q4 * (p4 * qp + 0.15 * qo) + 0.3 * p4 * po + floor
    )
    return scale_1, scale_2, scale_3, scale_4


def replay_kernel(zones, table_ref, tiles_ref, inverse_ref, sums_ref, raw_ref, second_ref, third_ref, to_odd, left_ref,
                  scales_ref, to_even, window):
    scales = scales_of(sums_ref[...], zones)
    for place, scale in enumerate(scales):
        scales_ref[place : place + 1, :] = jnp.broadcast_to(scale, (1, 128))
    inverse = inverse_ref[...]
    blocks = inverse.shape[0]
    a2 = 0.85 * scales[0]
    a3 = 0.85 * scales[1]

    def own_products(rows):
        spread_blocks(rows, left_ref)
        push_rows(table_ref, (OWN,), tiles_ref, left_ref, window, False)
        return jnp.sum(window[blocks : 2 * blocks], axis=1)

    def rounded(rows):
        return rows.astype(BF16).astype(F32)

    plain_2 = (raw_ref[...] * scales[0]) * inverse
    chain_2 = a2 * second_ref[0:blocks] + 0.15
    raw_2 = chain_2 + 0.85 * own_products(rounded(plain_2) - plain_2)
    chain_3 = a3 * (a2 * third_ref[0:blocks] + 0.15 * second_ref[blocks : 2 * blocks]) + 0.15
    weights_3 = rounded((raw_2 * scales[1]) * inverse)
    raw_3 = chain_3 + 0.85 * own_products(weights_3 - (chain_2 * scales[1]) * inverse)
    halo_step((raw_3 * scales[2]) * inverse, False, table_ref, tiles_ref, to_odd, left_ref, to_even, window)


def transposed_kernel(table_ref, tiles_ref, inverse_ref, scales_ref, odd, own, even, probe_ref, to_odd, to_even, pushed_ref, scaled_ref, root_ref, window):
    blocks, chans, width = pushed_ref.shape
    raw = 0.85 * (own[...] + odd[...] + even[...]) + 0.15
    root = jnp.sqrt(raw * scales_ref[3:4, 0:1])
    root_ref[...] = root
    inverse_root = 1.0 / root
    gain = root * inverse_ref[...]
    for block in range(blocks):
        probe = probe_ref[:, block * width : (block + 1) * width].astype(F32)
        pushed_ref[block] = (probe * gain[block : block + 1]).astype(BF16)
        scaled = (probe * inverse_root[block : block + 1]).astype(BF16)
        scaled_ref[block] = scaled
        to_odd[2 * blocks + block] = scaled
        to_even[2 * blocks + block] = scaled
    window[...] = jnp.zeros_like(window)

    def visit(tile, target):
        window[target] += jnp.dot(pushed_ref[tile >> 3], tiles_ref[tile], preferred_element_type=F32)

    for_tiles(table_ref, (ODD, EVEN), visit)
    for part, out in ((0, to_odd), (2, to_even)):
        for block in range(blocks):
            high, low = two_parts(window[part * blocks + block])
            out[block] = high.astype(BF16)
            out[blocks + block] = low.astype(BF16)


def own_products_kernel(table_ref, tiles_ref, pushed_ref, scaled_ref, kept, forward_ref, window, forward):
    blocks = pushed_ref.shape[0]
    window[...] = jnp.zeros_like(window)
    forward[...] = jnp.zeros_like(forward)

    def visit(tile, target):
        block = tile >> 3
        dead = target == DEAD
        place = jnp.where(dead, blocks, target - blocks)
        matrix = tiles_ref[tile]
        window[place] += jnp.dot(pushed_ref[block], matrix, preferred_element_type=F32)
        left = scaled_ref[jnp.where(dead, 0, place)]
        forward[jnp.where(dead, blocks, block)] += lax.dot_general(left, matrix, LAST_DIMS, preferred_element_type=F32)

    for_tiles(table_ref, (OWN,), visit)
    kept[...] = window[0:blocks]
    forward_ref[...] = forward[0:blocks]


def embed_kernel(table_ref, tiles_ref, inverse_ref, root_ref, kept, forward_ref, odd, even, out_ref, gram_ref, forward):
    blocks, chans, width = forward_ref.shape
    forward[0:blocks] = forward_ref[...]
    forward[blocks] = jnp.zeros((chans, width), F32)

    def visit(tile, target):
        dead = target == DEAD
        from_odd = odd[jnp.where(target < blocks, 2 * blocks + target, 2 * blocks)]
        from_even = even[jnp.where((target >= 2 * blocks) & (target < 3 * blocks), target, 2 * blocks)]
        left = jnp.where(target < blocks, from_odd, from_even)
        place = jnp.where(dead, blocks, tile >> 3)
        forward[place] += lax.dot_general(left, tiles_ref[tile], LAST_DIMS, preferred_element_type=F32)

    for_tiles(table_ref, (ODD, EVEN), visit)
    root = root_ref[...]
    inverse_root = 1.0 / root
    gain = root * inverse_ref[...]
    gram = jnp.zeros((chans, chans), F32)
    for block in range(blocks):
        landing = kept[block]
        for message in (odd, even):
            landing = landing + (message[block].astype(F32) + message[blocks + block].astype(F32))
        embedded = 0.5 * (forward[block] * gain[block : block + 1] + landing * inverse_root[block : block + 1])
        out_ref[:, block * width : (block + 1) * width] = embedded
        gram += lax.dot_general(embedded, embedded, LAST_DIMS, precision=HIGHEST, preferred_element_type=F32)
    gram_ref[...] = jnp.concatenate([gram[8 * i : 8 * i + 8] for i in range(4)], axis=1)


def basis_kernel(gram_ref, embedded_ref, out_hbm, out_ref, sems):
    size = embedded_ref.shape[0]
    row = lax.broadcasted_iota(jnp.int32, (size, size), 0)
    col = lax.broadcasted_iota(jnp.int32, (size, size), 1)
    identity = jnp.where(row == col, 1.0, 0.0)
    gram = jnp.sum(gram_ref[...], axis=0)
    gram = jnp.concatenate([gram[:, size * i : size * (i + 1)] for i in range(4)], axis=0)
    work = jnp.concatenate([gram, identity, jnp.zeros((size, 128 - 2 * size), F32)], axis=1)
    line = lax.broadcasted_iota(jnp.int32, work.shape, 0)
    for first in range(0, size, 16):
        columns = [jnp.broadcast_to(work[:, first + i : first + i + 1], work.shape) for i in range(16)]
        for i in range(16):
            step = first + i
            factor = jnp.where(line > step, columns[i] * (1.0 / columns[i][step : step + 1, :]), 0.0)
            work = work - factor * work[step : step + 1, :]
            for j in range(i + 1, 16):
                columns[j] = columns[j] - factor * columns[j][step : step + 1, :]
    pivots = jnp.sum(work[:, :size] * identity, axis=1, keepdims=True)
    inverse = work[:, size : 2 * size] * (1.0 / jnp.sqrt(pivots))
    parts = sems.shape[0]
    width = embedded_ref.shape[1] // parts
    copies = []
    for part in range(parts):
        span = pl.ds(part * width, width)
        out_ref[:, span] = jnp.dot(inverse, embedded_ref[:, span], precision=HIGHEST, preferred_element_type=F32)
        copies.append(pltpu.make_async_copy(out_ref.at[:, span], out_hbm.at[:, span], sems.at[part]))
        copies[-1].start()
    for copy in copies:
        copy.wait()


def call(kernel, name, outs, operands, specs, scratch, out_specs=None, limit=24, flops=0, moved=0):
    return pl.pallas_call(
        kernel,
        out_shape=outs,
        in_specs=specs,
        out_specs=out_specs or [VMEM] * len(outs),
        scratch_shapes=scratch,
        compiler_params=pltpu.CompilerParams(vmem_limit_bytes=limit << 20),
        cost_estimate=pl.CostEstimate(flops=flops, bytes_accessed=moved, transcendentals=0),
        name=name,
    )(*operands)


def per_device(tile_blocks, tile_cols, tile_count, start_mass, probe_block):
    blocks, slots, width = tile_blocks.shape[:3]
    chans = probe_block.shape[0]
    zones = blocks * lax.axis_size(RING) * width

    def rows(channels=1):
        return jax.ShapeDtypeStruct((channels * blocks, width), F32)

    def window(channels, kind=F32, places=3 * blocks + 1):
        return pltpu.VMEM((places, channels, width), kind)

    tiles, table, inverse, to_odd, left, to_even = call(
        load_kernel, "load",
        [
            pltpu.VMEM((blocks * slots, width, width), BF16), pltpu.SMEM((TABLE,), jnp.int32), rows(), rows(),
            jax.ShapeDtypeStruct((blocks, 16, width), BF16), rows(),
        ],
        [pltpu.with_memory_space_constraint(x, pltpu.HBM) for x in (tile_cols, tile_count, tile_blocks, start_mass)],
        [pl.BlockSpec(memory_space=pltpu.HBM)] * 4,
        [
            window(blocks), pltpu.VMEM((blocks, width), F32), pltpu.SMEM(tile_cols.shape, jnp.int32),
            pltpu.SMEM(tile_count.shape, jnp.int32), pltpu.SemaphoreType.DMA((blocks,)), pltpu.SemaphoreType.DMA((2 + blocks,)),
        ],
        [VMEM, SMEM, VMEM, VMEM, VMEM, VMEM],
    )
    tiles = pltpu.with_memory_space_constraint(tiles, pltpu.VMEM)
    table = pltpu.with_memory_space_constraint(table, pltpu.SMEM)

    def exchange(to_odd, left, name, channels, split, to_even=None):
        odd = swap_odd(to_odd)
        outs = [rows(channels)] * (1 if to_even is not None else 2)
        own, *made = call(
            functools.partial(own_kernel, split), name + "_own", outs, (table, tiles, left), [SMEM] + [VMEM] * 2,
            [window(channels * blocks)], flops=1 << 25, moved=1 << 22,
        )
        return odd, own, swap_even(made[0] if made else to_even)

    odd, own, even = exchange(to_odd, left, "first", 1, False, to_even)

    def step(kernel, name, channels, split, operands, extra, both):
        height = max(16, channels * blocks * (2 if split else 1))
        left = jax.ShapeDtypeStruct((blocks, height, width), BF16)
        to_odd, left, *extra = call(
            kernel, name, [rows(channels), left] + extra + [rows(channels)] * both, (table, tiles, inverse, *operands),
            [SMEM] + [VMEM] * (2 + len(operands)), [window(channels * blocks)], flops=1 << 24, moved=1 << 21,
        )
        to_even = extra.pop() if both else None
        return *exchange(to_odd, left, name, channels, split, to_even), *extra

    odd, own, even, raw = step(second_kernel, "second", 2, True, (odd, own, even), [rows()], False)
    odd, own, even, second = step(functools.partial(chain_kernel, 2), "third", 2, True, (odd, own, even), [rows(2)], False)
    odd, own, even, third = step(functools.partial(chain_kernel, 1), "fourth", 1, True, (odd, own, even), [rows(2)], True)
    (sums,) = call(
        sums_kernel, "sums", [jax.ShapeDtypeStruct((1, 128), F32)], (raw, second, third, odd, own, even), [VMEM] * 6, []
    )
    sums = chip_parts(sums[0])
    odd, own, even, scales = step(
        functools.partial(replay_kernel, zones), "replay", 1, False, (sums, raw, second, third),
        [jax.ShapeDtypeStruct((8, 128), F32)], True,
    )

    message = jax.ShapeDtypeStruct((3 * blocks, chans, width), BF16)
    narrow = jax.ShapeDtypeStruct((blocks, chans, width), BF16)
    wide = jax.ShapeDtypeStruct((blocks, chans, width), F32)
    to_odd, to_even, pushed, scaled, root = call(
        transposed_kernel, "transposed", [message, message, narrow, narrow, rows()],
        (table, tiles, inverse, scales, odd, own, even, probe_block), [SMEM] + [VMEM] * 7, [window(chans)],
    )
    odd, even = swap_odd(to_odd), swap_even(to_even)
    kept, forward = call(
        own_products_kernel, "own_products", [wide, wide], (table, tiles, pushed, scaled), [SMEM] + [VMEM] * 3,
        [window(chans, places=blocks + 1)] * 2, flops=1 << 28, moved=1 << 23,
    )
    embedded, gram = call(
        embed_kernel, "embed",
        [jax.ShapeDtypeStruct((chans, blocks * width), F32), jax.ShapeDtypeStruct((8, 128), F32)],
        (table, tiles, inverse, root, kept, forward, odd, even), [SMEM] + [VMEM] * 7, [window(chans, places=blocks + 1)],
    )
    (basis,) = call(
        basis_kernel, "basis", [pltpu.HBM((chans, blocks * width), F32)], (plane_parts(gram), embedded), [VMEM] * 2,
        [pltpu.VMEM((chans, blocks * width), F32), pltpu.SemaphoreType.DMA((4,))], [pl.BlockSpec(memory_space=pltpu.HBM)],
    )
    return basis


def solution(mesh):
    return jax.shard_map(
        per_device,
        mesh=mesh,
        in_specs=(P(RING, None, None, None), P(RING, None), P(RING), P(RING), P(None, RING)),
        out_specs=P(None, RING),
        check_vma=False,
    )
```

```python
import functools
import math

import jax
import jax.numpy as jnp
from jax import lax
from jax.experimental import pallas as pl
from jax.experimental.pallas import tpu as pltpu
from jax.sharding import PartitionSpec as P

RING = ("rows", "cols")
F32 = jnp.float32
BF16 = jnp.bfloat16
HIGHEST = lax.Precision.HIGHEST
LAST_DIMS = (((1,), (1,)), ((), ()))
SMEM = pl.BlockSpec(memory_space=pltpu.SMEM)
VMEM = pl.BlockSpec(memory_space=pltpu.VMEM)
CHUNK = 8
DEAD = 24
HALO_CHUNKS = 128
OWN_CHUNKS = 129
SPARE = 130


def swap(shard, axis, partner):
    count = lax.axis_size(axis)
    return lax.ppermute(shard, axis, [(i, partner(i) % count) for i in range(count)])


def ring_pairs(shard_odd, shard_even):
    got_odd = swap(shard_odd, RING, lambda i: i + 1 if i % 2 else i - 1)
    got_even = swap(shard_even, RING, lambda i: i - 1 if i % 2 else i + 1)
    return got_odd, got_even


def gathered(part, axis, groups):
    spread = jnp.broadcast_to(part[None], (len(groups[0]), *part.shape))
    return lax.all_to_all(spread, axis, 0, 0, tiled=True, axis_index_groups=groups)


def chip_parts(part):
    part = part + swap(part, "rows", lambda i: i ^ 1)
    cols = lax.axis_size("cols")
    devices = lax.axis_size(RING)
    groups = [[i for i in range(devices) if (i // cols) % 2 == core] for core in (0, 1)]
    return gathered(part, RING, groups)


def plane_parts(part):
    part = part + swap(part, "rows", lambda i: i ^ 1)
    part = part + sum(swap(part, "cols", lambda i, d=d: i ^ d) for d in (1, 2, 3))
    groups = [list(range(core, lax.axis_size("rows"), 2)) for core in (0, 1)]
    return gathered(part, "rows", groups)


def two_parts(value):
    high = value.astype(BF16).astype(F32)
    return high, value - high


def spread_blocks(rows, left_ref):
    blocks, height = left_ref.shape[:2]
    if rows.shape[0] < height:
        rows = jnp.concatenate([rows, jnp.zeros((height - rows.shape[0], rows.shape[1]), F32)], axis=0)
    owner = lax.broadcasted_iota(jnp.int32, rows.shape, 0) % blocks
    for block in range(blocks):
        left_ref[block] = jnp.where(owner == block, rows, 0.0).astype(BF16)


def for_tiles(table_ref, own, visit):
    first = 64 if own else 0

    def chunk(number, carry):
        for place in range(CHUNK):
            entry = table_ref[first + number * CHUNK + place]
            visit(entry >> 5, entry & 31)
        return carry

    lax.fori_loop(0, table_ref[OWN_CHUNKS if own else HALO_CHUNKS], chunk, 0)


def push_rows(table_ref, own, tiles_ref, left_ref, window, split):
    height = window.shape[1]
    window[...] = jnp.zeros_like(window)

    def visit(tile, target):
        product = jnp.dot(left_ref[tile >> 3], tiles_ref[tile], preferred_element_type=F32)
        if split:
            product = product[:height] + product[height : 2 * height]
        window[target] += product[:height]

    for_tiles(table_ref, own, visit)


def landed(window, part, out):
    for channel in range(out.shape[0] // 8):
        rows = slice(channel * 8, (channel + 1) * 8)
        out[rows, :] = jnp.sum(window[part * 8 : (part + 1) * 8, rows, :], axis=1)


def load_kernel(cols_hbm, count_hbm, tiles_hbm, start_hbm, tiles_ref, table_ref, inverse_ref, to_odd, to_even, left_ref,
                window, start_ref, cols_ref, count_ref, sems, small_sems):
    blocks, slots, width = tiles_hbm.shape[:3]
    small = [
        pltpu.make_async_copy(cols_hbm, cols_ref, small_sems.at[0]),
        pltpu.make_async_copy(count_hbm, count_ref, small_sems.at[1]),
    ]
    small += [
        pltpu.make_async_copy(start_hbm.at[pl.ds(b * width, width)], start_ref.at[b], small_sems.at[2 + b]) for b in range(blocks)
    ]
    copies = [
        pltpu.make_async_copy(tiles_hbm.at[b], tiles_ref.at[pl.ds(b * slots, slots)], sems.at[b]) for b in range(blocks)
    ]
    for copy in small + copies:
        copy.start()
    total_blocks = blocks * lax.axis_size("rows") * lax.axis_size("cols")
    place = lax.axis_index("rows") * lax.axis_size("cols") + lax.axis_index("cols")
    swapped = place % 2 == 1
    for entry in range(128):
        table_ref[entry] = DEAD
    for copy in small:
        copy.wait()
    halo_count, own_count = jnp.int32(0), jnp.int32(0)
    for block in range(blocks):
        for slot in range(slots):
            target = cols_ref[block, slot] - place * blocks + blocks
            target = jnp.where(target < 0, target + total_blocks, target)
            target = jnp.where(target >= total_blocks, target - total_blocks, target)
            own = (target >= blocks) & (target < 2 * blocks)
            flipped = jnp.where(target < blocks, target + 2 * blocks, target - 2 * blocks)
            target = jnp.where(swapped & jnp.logical_not(own), flipped, target)
            live = slot < count_ref[block]
            to_own = live & own
            to_halo = live & jnp.logical_not(own)
            entry = target + (block * slots + slot) * 32
            table_ref[jnp.where(to_halo, halo_count, jnp.where(to_own, 64 + own_count, SPARE))] = entry
            halo_count += jnp.where(to_halo, 1, 0)
            own_count += jnp.where(to_own, 1, 0)
    table_ref[HALO_CHUNKS] = (halo_count + CHUNK - 1) >> 3
    table_ref[OWN_CHUNKS] = (own_count + CHUNK - 1) >> 3

    ones = jnp.ones((16, 128), BF16)

    def folded_tiles(block):
        folded = jnp.zeros((width, 128), F32)
        for slot in range(slots):
            tile = tiles_ref[block * slots + slot].astype(F32)
            folded = folded + (tile[:, :128] + tile[:, 128:]) * jnp.where(slot < count_ref[block], 1.0, 0.0)
        return folded

    def row_sums(folded):
        total = jnp.zeros((16, width), F32)
        for _ in range(3):
            part = folded.astype(BF16)
            folded = folded - part.astype(F32)
            total = total + lax.dot_general(ones, part, LAST_DIMS, preferred_element_type=F32)
        return total[0:1]

    sums = []
    before = None
    for block in range(blocks):
        copies[block].wait()
        folded = folded_tiles(block)
        if before is not None:
            sums.append(row_sums(before))
        before = folded
    sums.append(row_sums(before))
    inverse = 1.0 / jnp.concatenate(sums, axis=0)
    inverse_ref[...] = inverse
    halo_step(start_ref[...] * inverse, False, table_ref, tiles_ref, to_odd, to_even, left_ref, window)


def halo_step(rows, split, table_ref, tiles_ref, to_odd, to_even, left_ref, window):
    spread_blocks(jnp.concatenate(two_parts(rows), axis=0) if split else rows, left_ref)
    push_rows(table_ref, False, tiles_ref, left_ref, window, split)
    landed(window, 0, to_odd)
    landed(window, 2, to_even)


def second_kernel(table_ref, tiles_ref, inverse_ref, odd, own, even, to_odd, to_even, left_ref, value_ref, window):
    raw = 0.85 * (own[...] + odd[...] + even[...]) + 0.15
    value_ref[...] = raw
    inverse = inverse_ref[...]
    rows = jnp.concatenate([raw * inverse, inverse], axis=0)
    halo_step(rows, True, table_ref, tiles_ref, to_odd, to_even, left_ref, window)


def chain_kernel(channels, table_ref, tiles_ref, inverse_ref, odd, own, even, to_odd, to_even, left_ref, value_ref, window):
    value = own[...] + odd[...] + even[...]
    value_ref[...] = value
    inverse = inverse_ref[...]
    rows = [value[8 * c : 8 * c + 8] * inverse for c in range(channels)]
    rows = jnp.concatenate(rows, axis=0) if channels > 1 else rows[0]
    halo_step(rows, True, table_ref, tiles_ref, to_odd, to_even, left_ref, window)


def own_kernel(split, table_ref, tiles_ref, left_ref, kept, window):
    push_rows(table_ref, True, tiles_ref, left_ref, window, split)
    landed(window, 1, kept)


def sums_kernel(raw_ref, second_ref, third_ref, odd, own, even, out_ref):
    raw = raw_ref[...]
    second = second_ref[0:8]
    ones_1 = second_ref[8:16]
    third = third_ref[0:8]
    ones_2 = third_ref[8:16]
    fourth = own[...] + odd[...] + even[...]
    wanted = (
        raw * raw,
        second * second, second,
        third * third, third * ones_1, third, ones_1 * ones_1, ones_1,
        fourth * fourth, fourth * ones_2, fourth * ones_1, fourth,
        ones_2 * ones_2, ones_2 * ones_1, ones_2, jnp.zeros_like(raw),
    )
    lines = [jnp.sum(term[:, :128] + term[:, 128:], axis=0, keepdims=True) for term in wanted]
    lines = jnp.sum(jnp.concatenate(lines, axis=0), axis=1, keepdims=True)
    row = lax.broadcasted_iota(jnp.int32, (16, 128), 0)
    lane = lax.broadcasted_iota(jnp.int32, (16, 128), 1)
    out_ref[...] = jnp.sum(jnp.where(row == lane, lines, 0.0), axis=0, keepdims=True)


def scales_of(sums, zones):
    line = jnp.broadcast_to(jnp.sum(sums, axis=0, keepdims=True), (16, 128))
    row = lax.broadcasted_iota(jnp.int32, line.shape, 0)
    lane = lax.broadcasted_iota(jnp.int32, line.shape, 1)
    totals = jnp.sum(jnp.where(row == lane, line, 0.0), axis=1, keepdims=True)
    (r11, c22, c2o, c33, c3p, c3o, pp, po, c44, c4q, c4p, c4o, qq, qp, qo) = (totals[i : i + 1] for i in range(15))
    root = math.sqrt(zones)
    floor = 0.15 * 0.15 * zones
    scale_1 = root / jnp.sqrt(r11)
    a2 = 0.85 * scale_1
    scale_2 = root / jnp.sqrt(a2 * a2 * c22 + 0.3 * a2 * c2o + floor)
    a3 = 0.85 * scale_2 * a2
    p3 = 0.85 * scale_2 * 0.15
    scale_3 = root / jnp.sqrt(
        a3 * a3 * c33 + 2.0 * a3 * (p3 * c3p + 0.15 * c3o) + p3 * p3 * pp + 0.3 * p3 * po + floor
    )
    a4 = 0.85 * scale_3 * a3
    q4 = 0.85 * scale_3 * p3
    p4 = 0.85 * scale_3 * 0.15
    scale_4 = root / jnp.sqrt(
        a4 * a4 * c44 + 2.0 * a4 * (q4 * c4q + p4 * c4p + 0.15 * c4o)
        + q4 * q4 * qq + p4 * p4 * pp + 2.0 * q4 * (p4 * qp + 0.15 * qo) + 0.3 * p4 * po + floor
    )
    return scale_1, scale_2, scale_3, scale_4


def replay_kernel(zones, table_ref, tiles_ref, inverse_ref, sums_ref, raw_ref, second_ref, third_ref, to_odd, to_even, left_ref,
                  scales_ref, window):
    scales = scales_of(sums_ref[...], zones)
    for place, scale in enumerate(scales):
        scales_ref[place : place + 1, :] = jnp.broadcast_to(scale, (1, 128))
    inverse = inverse_ref[...]
    blocks = inverse.shape[0]
    a2 = 0.85 * scales[0]
    a3 = 0.85 * scales[1]

    def own_products(rows):
        spread_blocks(rows, left_ref)
        push_rows(table_ref, True, tiles_ref, left_ref, window, False)
        return jnp.sum(window[blocks : 2 * blocks], axis=1)

    def rounded(rows):
        return rows.astype(BF16).astype(F32)

    plain_2 = (raw_ref[...] * scales[0]) * inverse
    chain_2 = a2 * second_ref[0:blocks] + 0.15
    raw_2 = chain_2 + 0.85 * own_products(rounded(plain_2) - plain_2)
    chain_3 = a3 * (a2 * third_ref[0:blocks] + 0.15 * second_ref[blocks : 2 * blocks]) + 0.15
    weights_3 = rounded((raw_2 * scales[1]) * inverse)
    raw_3 = chain_3 + 0.85 * own_products(weights_3 - (chain_2 * scales[1]) * inverse)
    halo_step((raw_3 * scales[2]) * inverse, False, table_ref, tiles_ref, to_odd, to_even, left_ref, window)


def transposed_kernel(table_ref, tiles_ref, inverse_ref, scales_ref, odd, own, even, probe_ref, to_odd, to_even, pushed_ref, scaled_ref, root_ref, window):
    blocks, chans, width = pushed_ref.shape
    raw = 0.85 * (own[...] + odd[...] + even[...]) + 0.15
    root = jnp.sqrt(raw * scales_ref[3:4, 0:1])
    root_ref[...] = root
    inverse_root = 1.0 / root
    gain = root * inverse_ref[...]
    for block in range(blocks):
        probe = probe_ref[:, block * width : (block + 1) * width].astype(F32)
        pushed_ref[block] = (probe * gain[block : block + 1]).astype(BF16)
        scaled = (probe * inverse_root[block : block + 1]).astype(BF16)
        scaled_ref[block] = scaled
        to_odd[2 * blocks + block] = scaled
        to_even[2 * blocks + block] = scaled
    window[...] = jnp.zeros_like(window)

    def visit(tile, target):
        window[target] += jnp.dot(pushed_ref[tile >> 3], tiles_ref[tile], preferred_element_type=F32)

    for_tiles(table_ref, False, visit)
    for part, out in ((0, to_odd), (2, to_even)):
        for block in range(blocks):
            high, low = two_parts(window[part * blocks + block])
            out[block] = high.astype(BF16)
            out[blocks + block] = low.astype(BF16)


def own_products_kernel(table_ref, tiles_ref, inverse_ref, root_ref, pushed_ref, scaled_ref, base_ref, window, forward):
    blocks = pushed_ref.shape[0]
    window[...] = jnp.zeros_like(window)
    forward[...] = jnp.zeros_like(forward)

    def visit(tile, target):
        block = tile >> 3
        dead = target == DEAD
        place = jnp.where(dead, blocks, target - blocks)
        matrix = tiles_ref[tile]
        window[place] += jnp.dot(pushed_ref[block], matrix, preferred_element_type=F32)
        left = scaled_ref[jnp.where(dead, 0, place)]
        forward[jnp.where(dead, blocks, block)] += lax.dot_general(left, matrix, LAST_DIMS, preferred_element_type=F32)

    for_tiles(table_ref, True, visit)
    root = root_ref[...]
    inverse_root = 1.0 / root
    gain = root * inverse_ref[...]
    for block in range(blocks):
        line = slice(block, block + 1)
        base_ref[block] = 0.5 * (forward[block] * gain[line] + window[block] * inverse_root[line])


def embed_kernel(table_ref, tiles_ref, inverse_ref, root_ref, base_ref, odd, even, out_ref, gram_ref, forward):
    blocks, chans, width = base_ref.shape
    forward[...] = jnp.zeros_like(forward)

    def visit(tile, target):
        dead = target == DEAD
        from_odd = odd[jnp.where(target < blocks, 2 * blocks + target, 2 * blocks)]
        from_even = even[jnp.where((target >= 2 * blocks) & (target < 3 * blocks), target, 2 * blocks)]
        left = jnp.where(target < blocks, from_odd, from_even)
        place = jnp.where(dead, blocks, tile >> 3)
        forward[place] += lax.dot_general(left, tiles_ref[tile], LAST_DIMS, preferred_element_type=F32)

    for_tiles(table_ref, False, visit)
    root = root_ref[...]
    inverse_root = 1.0 / root
    gain = root * inverse_ref[...]
    gram = jnp.zeros((chans, chans), F32)
    for block in range(blocks):
        landing = odd[block].astype(F32) + odd[blocks + block].astype(F32)
        landing = landing + (even[block].astype(F32) + even[blocks + block].astype(F32))
        arrived = forward[block] * gain[block : block + 1] + landing * inverse_root[block : block + 1]
        embedded = base_ref[block] + 0.5 * arrived
        out_ref[:, block * width : (block + 1) * width] = embedded
        gram += lax.dot_general(embedded, embedded, LAST_DIMS, precision=HIGHEST, preferred_element_type=F32)
    gram_ref[...] = jnp.concatenate([gram[8 * i : 8 * i + 8] for i in range(4)], axis=1)


def basis_kernel(gram_ref, embedded_ref, out_hbm, out_ref, sems):
    size = embedded_ref.shape[0]
    row = lax.broadcasted_iota(jnp.int32, (size, size), 0)
    col = lax.broadcasted_iota(jnp.int32, (size, size), 1)
    identity = jnp.where(row == col, 1.0, 0.0)
    gram = jnp.sum(gram_ref[...], axis=0)
    gram = jnp.concatenate([gram[:, size * i : size * (i + 1)] for i in range(4)], axis=0)
    work = jnp.concatenate([gram, identity, jnp.zeros((size, 128 - 2 * size), F32)], axis=1)
    line = lax.broadcasted_iota(jnp.int32, work.shape, 0)
    for first in range(0, size, 16):
        columns = [jnp.broadcast_to(work[:, first + i : first + i + 1], work.shape) for i in range(16)]
        for i in range(16):
            step = first + i
            factor = jnp.where(line > step, columns[i] * (1.0 / columns[i][step : step + 1, :]), 0.0)
            work = work - factor * work[step : step + 1, :]
            for j in range(i + 1, 16):
                columns[j] = columns[j] - factor * columns[j][step : step + 1, :]
    pivots = jnp.sum(work[:, :size] * identity, axis=1, keepdims=True)
    inverse = work[:, size : 2 * size] * (1.0 / jnp.sqrt(pivots))
    parts = sems.shape[0]
    width = embedded_ref.shape[1] // parts
    copies = []
    for part in range(parts):
        span = pl.ds(part * width, width)
        out_ref[:, span] = jnp.dot(inverse, embedded_ref[:, span], precision=HIGHEST, preferred_element_type=F32)
        copies.append(pltpu.make_async_copy(out_ref.at[:, span], out_hbm.at[:, span], sems.at[part]))
        copies[-1].start()
    for copy in copies:
        copy.wait()


def call(kernel, name, outs, operands, specs, scratch, out_specs=None, limit=24, flops=0, moved=0):
    return pl.pallas_call(
        kernel,
        out_shape=outs,
        in_specs=specs,
        out_specs=out_specs or [VMEM] * len(outs),
        scratch_shapes=scratch,
        compiler_params=pltpu.CompilerParams(vmem_limit_bytes=limit << 20),
        cost_estimate=pl.CostEstimate(flops=flops, bytes_accessed=moved, transcendentals=0),
        name=name,
    )(*operands)


def per_device(tile_blocks, tile_cols, tile_count, start_mass, probe_block):
    blocks, slots, width = tile_blocks.shape[:3]
    chans = probe_block.shape[0]
    zones = blocks * lax.axis_size(RING) * width

    def rows(channels=1):
        return jax.ShapeDtypeStruct((channels * blocks, width), F32)

    def window(channels, kind=F32, places=3 * blocks + 1):
        return pltpu.VMEM((places, channels, width), kind)

    tiles, table, inverse, to_odd, to_even, left = call(
        load_kernel, "load",
        [
            pltpu.VMEM((blocks * slots, width, width), BF16), pltpu.SMEM((136,), jnp.int32), rows(), rows(), rows(),
            jax.ShapeDtypeStruct((blocks, 16, width), BF16),
        ],
        [pltpu.with_memory_space_constraint(x, pltpu.HBM) for x in (tile_cols, tile_count, tile_blocks, start_mass)],
        [pl.BlockSpec(memory_space=pltpu.HBM)] * 4,
        [
            window(blocks), pltpu.VMEM((blocks, width), F32), pltpu.SMEM(tile_cols.shape, jnp.int32),
            pltpu.SMEM(tile_count.shape, jnp.int32), pltpu.SemaphoreType.DMA((blocks,)), pltpu.SemaphoreType.DMA((2 + blocks,)),
        ],
        [VMEM, SMEM, VMEM, VMEM, VMEM, VMEM],
    )
    tiles = pltpu.with_memory_space_constraint(tiles, pltpu.VMEM)
    table = pltpu.with_memory_space_constraint(table, pltpu.SMEM)

    def exchange(to_odd, to_even, left, name, channels, split):
        odd, even = ring_pairs(to_odd, to_even)
        (own,) = call(
            functools.partial(own_kernel, split), name + "_own", [rows(channels)], (table, tiles, left), [SMEM] + [VMEM] * 2,
            [window(channels * blocks)], flops=1 << 25, moved=1 << 22,
        )
        return odd, own, even

    odd, own, even = exchange(to_odd, to_even, left, "first", 1, False)

    def step(kernel, name, channels, split, operands, extra):
        height = max(16, channels * blocks * (2 if split else 1))
        left = jax.ShapeDtypeStruct((blocks, height, width), BF16)
        to_odd, to_even, left, *extra = call(
            kernel, name, [rows(channels)] * 2 + [left] + extra, (table, tiles, inverse, *operands),
            [SMEM] + [VMEM] * (2 + len(operands)), [window(channels * blocks)], flops=1 << 24, moved=1 << 21,
        )
        return *exchange(to_odd, to_even, left, name, channels, split), *extra

    odd, own, even, raw = step(second_kernel, "second", 2, True, (odd, own, even), [rows()])
    odd, own, even, second = step(functools.partial(chain_kernel, 2), "third", 2, True, (odd, own, even), [rows(2)])
    odd, own, even, third = step(functools.partial(chain_kernel, 1), "fourth", 1, True, (odd, own, even), [rows(2)])
    (sums,) = call(
        sums_kernel, "sums", [jax.ShapeDtypeStruct((1, 128), F32)], (raw, second, third, odd, own, even), [VMEM] * 6, []
    )
    sums = chip_parts(sums[0])
    odd, own, even, scales = step(
        functools.partial(replay_kernel, zones), "replay", 1, False, (sums, raw, second, third),
        [jax.ShapeDtypeStruct((8, 128), F32)],
    )

    message = jax.ShapeDtypeStruct((3 * blocks, chans, width), BF16)
    narrow = jax.ShapeDtypeStruct((blocks, chans, width), BF16)
    wide = jax.ShapeDtypeStruct((blocks, chans, width), F32)
    to_odd, to_even, pushed, scaled, root = call(
        transposed_kernel, "transposed", [message, message, narrow, narrow, rows()],
        (table, tiles, inverse, scales, odd, own, even, probe_block), [SMEM] + [VMEM] * 7, [window(chans)],
    )
    odd, even = ring_pairs(to_odd, to_even)
    (base,) = call(
        own_products_kernel, "own_products", [wide], (table, tiles, inverse, root, pushed, scaled), [SMEM] + [VMEM] * 5,
        [window(chans, places=blocks + 1)] * 2, flops=1 << 28, moved=1 << 23,
    )
    embedded, gram = call(
        embed_kernel, "embed",
        [jax.ShapeDtypeStruct((chans, blocks * width), F32), jax.ShapeDtypeStruct((8, 128), F32)],
        (table, tiles, inverse, root, base, odd, even), [SMEM] + [VMEM] * 6, [window(chans, places=blocks + 1)],
    )
    (basis,) = call(
        basis_kernel, "basis", [pltpu.HBM((chans, blocks * width), F32)], (plane_parts(gram), embedded), [VMEM] * 2,
        [pltpu.VMEM((chans, blocks * width), F32), pltpu.SemaphoreType.DMA((4,))], [pl.BlockSpec(memory_space=pltpu.HBM)],
    )
    return basis


def solution(mesh):
    return jax.shard_map(
        per_device,
        mesh=mesh,
        in_specs=(P(RING, None, None, None), P(RING, None), P(RING), P(RING), P(None, RING)),
        out_specs=P(None, RING),
        check_vma=False,
    )
```
